32 devices in a mesh: expert: 8 (over z, x), dp: 4 (over y, core).
Axes of the slice: x: 2, y: 2, z: 4, core: 2. Of those that a mesh axis runs over, the one named last changes fastest.
Arguments:
- tokens: bfloat16 [1024, 3584], P('expert', 'dp'), may hold values from -6 to 6
- route_ids: int32 [1024, 8], P('expert'), may hold values from 0 to 7, as said below
- gate_scores: float32 [1024, 8], P('expert'), may hold values from 0.1 to 1, as said below
- up_weight: bfloat16 [8, 3584, 1024], P('expert', 'dp'), may hold values from -0.09375 to 0.09375
- down_weight: bfloat16 [8, 1024, 3584], P('expert', None, 'dp'), may hold values from -0.1875 to 0.1875
Outputs:
- mixed: bfloat16 [1024, 3584], P('expert', 'dp')
The draws below stay inside these ranges and needn't reach their ends.
Inputs may be any that keep to these rules, and one draw needn't show every extreme that they name: `route_ids`: each row names 8 different experts. The same 2 experts are named by exactly 128 rows in every aligned block of 128 rows (the tokens of one device); in such a block every other expert is named by 128 - 1 or 128 rows. `gate_scores`: positive affinities.
All inputs are finite; a program needn't handle non-finite values.
Results may differ from the reference program's by a relative error of at most 0.017.
Values may be sent and summed in bfloat16 or wider, within the bound.
A program may use at most 64 MiB of HBM per device.

```python
import jax
import jax.numpy as jnp
from jax import lax

D = 3584
HID = 1024
TOP = 8
HOT = 2
TOK_DEV = 128
EXPERTS = 8
TOKENS = 1024
HOT_MOST = 128
COLD_MOST = 128
N_EXPERT = 8
N_DP = 4


def route_table(key):
    blocks = TOKENS // TOK_DEV
    mean_rows = TOK_DEV * TOP // EXPERTS
    cold_rows = (EXPERTS - HOT) * mean_rows - HOT * (HOT_MOST - mean_rows)
    base_count = cold_rows // (EXPERTS - HOT)
    extra_count = cold_rows % (EXPERTS - HOT)
    expert_order = jax.random.permutation(jax.random.fold_in(key, 11), EXPERTS).astype(jnp.int32)

    def one_block(block_index):
        block_key = jax.random.fold_in(key, block_index)
        cold_list = jax.random.permutation(jax.random.fold_in(block_key, 1), expert_order[HOT:])
        listed = jnp.concatenate([expert_order[:HOT], cold_list]).astype(jnp.int32)
        counts = jnp.concatenate([jnp.full((HOT,), HOT_MOST, jnp.int32), jnp.where(jnp.arange(EXPERTS - HOT) < extra_count, base_count + 1, base_count).astype(jnp.int32)])
        bounds = jnp.cumsum(counts).astype(jnp.int32)
        position = jnp.arange(TOK_DEV * TOP, dtype=jnp.int32)
        owner_index = jnp.sum((position[:, None] >= bounds[None, :]).astype(jnp.int32), axis=1)
        sequence = listed[owner_index]
        layout = sequence.reshape(TOP, TOK_DEV).T
        shuffle = jax.random.permutation(jax.random.fold_in(block_key, 2), TOK_DEV)
        layout = layout[shuffle]
        sort_keys = jax.random.randint(jax.random.fold_in(block_key, 3), (TOK_DEV, TOP), 0, 1 << 20) * TOP
        sort_keys = sort_keys + jnp.arange(TOP, dtype=jnp.int32)[None, :]
        order_cols = jnp.argsort(sort_keys, axis=1)
        return jnp.take_along_axis(layout, order_cols, axis=1)
    drawn = jax.vmap(one_block)(jnp.arange(blocks, dtype=jnp.int32))
    return (drawn.reshape(TOKENS, TOP).astype(jnp.int32), expert_order[:HOT])


def draw_route_ids(key, part):
    route_rows, hot_list = route_table(key)
    return route_rows


def draw_gate_scores(key, part):
    route_rows, hot_list = route_table(key)
    hot_mask = jnp.any(route_rows[:, :, None] == hot_list[None, None, :], axis=2)
    score_key = jax.random.fold_in(key, 1000003)
    upper_key = jax.random.fold_in(score_key, 1)
    lower_key = jax.random.fold_in(score_key, 2)
    hot_values = jnp.exp(jax.random.uniform(upper_key, (TOKENS, TOP), jnp.float32, jnp.log(0.6), 0.0))
    cold_values = jnp.exp(jax.random.uniform(lower_key, (TOKENS, TOP), jnp.float32, jnp.log(0.1), jnp.log(0.4)))
    scores = jnp.where(hot_mask, hot_values, cold_values)
    return jnp.clip(scores, 0.1, 1.0).astype(jnp.float32)


def steps_of(own_key, dims, shards, smallest, top_value):
    level = 1.0
    for dim, blocks in shards:
        heights = jax.random.uniform(jax.random.fold_in(jax.random.fold_in(own_key, 6), dim), (blocks,), jnp.float32, smallest / len(shards), top_value / len(shards))
        level = level * jnp.repeat(jnp.exp(heights), dims[dim] // blocks).reshape((-1,) + (1,) * (len(dims) - 1 - dim))
    return level


def normal_values(key, extent, width, bound, shards=(), kind=jnp.bfloat16):
    entries = width * jax.random.normal(key, extent, jnp.float32)
    if shards:
        entries = entries * steps_of(key, extent, shards, -0.22, 0.18)
    return jnp.clip(entries, -bound, bound).astype(kind)


def setup_inputs(seed: int = 0) -> dict:
    arg_keys = jax.random.split(jax.random.key(seed), 6)
    tokens = normal_values(arg_keys[0], (TOKENS, D), 1.0, 6.0, ((0, 8), (1, 4)))
    route_ids = draw_route_ids(jax.random.fold_in(arg_keys[5], 71), 0)
    gate_scores = draw_gate_scores(jax.random.fold_in(arg_keys[5], 71), 0)
    up_weight = normal_values(arg_keys[3], (EXPERTS, D, HID), D ** -0.5, 0.09375, ((0, 8), (1, 4)))
    down_weight = normal_values(arg_keys[4], (EXPERTS, HID, D), HID ** -0.5, 0.1875, ((0, 8), (2, 4)))
    return {"tokens": tokens, "route_ids": route_ids, "gate_scores": gate_scores, "up_weight": up_weight, "down_weight": down_weight}


ROUTE_SCALE = 2.5


def reference(tokens, route_ids, gate_scores, up_weight, down_weight):
    row_total = TOKENS * TOP
    flat_ids = route_ids.reshape(-1).astype(jnp.int32)
    mix_weights = gate_scores * (ROUTE_SCALE / jnp.sum(gate_scores, axis=1, keepdims=True))
    flat_weights = jnp.concatenate([mix_weights.reshape(-1), jnp.zeros((1,), jnp.float32)])
    onehot = (flat_ids[:, None] == jnp.arange(EXPERTS, dtype=jnp.int32)[None, :]).astype(jnp.int32)
    running = (jnp.cumsum(onehot, axis=0) - 1).astype(jnp.int32)
    row_ranks = jnp.sum(onehot * running, axis=1).astype(jnp.int32)
    capacity = N_EXPERT * max(HOT_MOST, COLD_MOST)
    slot_table = jnp.full((EXPERTS, capacity), row_total, jnp.int32)
    slot_table = slot_table.at[flat_ids, row_ranks].set(jnp.arange(row_total, dtype=jnp.int32))
    padded = jnp.concatenate([tokens, jnp.zeros((1, D), jnp.bfloat16)], axis=0)
    piece_width = D // N_DP

    def one_expert(totals, inputs):
        slot_rows, up_one, down_one = inputs
        token_rows = (slot_rows // TOP).astype(jnp.int32)
        gathered = padded[token_rows]
        pieces = jnp.einsum("rpc,pch->rph",
                            gathered.reshape(capacity, N_DP, piece_width).astype(jnp.float32),
                            up_one.reshape(N_DP, piece_width, HID).astype(jnp.float32))
        rounded = lax.optimization_barrier(pieces.astype(jnp.bfloat16)).astype(jnp.float32)
        before = jnp.sum(rounded, axis=1)
        hidden = jax.nn.silu(before).astype(jnp.bfloat16)
        output = jnp.dot(hidden, down_one, preferred_element_type=jnp.float32)
        output_rounded = lax.optimization_barrier(output.astype(jnp.bfloat16)).astype(jnp.float32)
        weights = flat_weights[slot_rows]
        totals = totals.at[token_rows].add(weights[:, None] * output_rounded)
        return totals, None

    start = jnp.zeros((TOKENS + 1, D), jnp.float32)
    result, unused = lax.scan(one_expert, start, (slot_table, up_weight, down_weight))
    return result[:TOKENS].astype(jnp.bfloat16)
```

```python
import functools

import jax
import jax.numpy as jnp
from jax import lax
from jax.experimental import pallas as pl
from jax.experimental.pallas import tpu as pltpu
from jax.sharding import PartitionSpec as P

HOT = 2


ROUTE_SCALE = 2.5


def silu_hidden(before):
    summed = lax.psum(before.astype(jnp.bfloat16), "dp").astype(jnp.float32)
    result = jax.nn.silu(summed).astype(jnp.bfloat16)
    return result


def routed(tokens, route_ids, gate_scores, up_weight, down_weight):
    token_count, chosen_count = route_ids.shape
    features = tokens.shape[1]
    experts = lax.axis_size("expert")
    mean_rows = token_count * chosen_count // experts
    hot_most = min(2 * mean_rows - 1, token_count)
    cold_rows = (experts - HOT) * mean_rows - HOT * (hot_most - mean_rows)
    cold_most = -(-cold_rows // (experts - HOT))
    flat_ids = route_ids.reshape(-1)
    row_total = flat_ids.shape[0]
    expert_range = jnp.arange(experts, dtype=jnp.int32)
    onehot = (flat_ids[:, None] == expert_range[None, :]).astype(jnp.int32)
    running = jnp.cumsum(onehot, axis=0) - 1
    row_ranks = jnp.sum(onehot * running, axis=1)
    padded = jnp.concatenate([tokens, jnp.zeros((1, features), tokens.dtype)], axis=0)
    up_local = up_weight[0]
    down_local = down_weight[0]
    mix_weights = gate_scores * (ROUTE_SCALE / jnp.sum(gate_scores, axis=1, keepdims=True))
    slot_count = max(hot_most, cold_most)
    slot_of_row = flat_ids * slot_count + row_ranks
    slot_table = jnp.full((experts * slot_count,), row_total, jnp.int32)
    slot_table = slot_table.at[slot_of_row].set(jnp.arange(row_total, dtype=jnp.int32), mode="drop")
    sending = padded[slot_table // chosen_count].reshape(experts, slot_count, features)
    arrived = lax.all_to_all(sending, "expert", split_axis=0, concat_axis=0, tiled=True)
    item_count = arrived.shape[1]
    flat_rows = arrived.reshape(-1, features)
    before = jnp.dot(flat_rows, up_local, preferred_element_type=jnp.float32)
    hidden = silu_hidden(before)
    output = jnp.dot(hidden, down_local, preferred_element_type=jnp.float32)
    outcome = output.astype(jnp.bfloat16).reshape(experts, item_count, features)
    returned = lax.all_to_all(outcome, "expert", split_axis=0, concat_axis=0, tiled=True).reshape(
        -1, features
    )
    picked = returned[slot_of_row]
    picked = picked.reshape(token_count, chosen_count, features).astype(jnp.float32)
    mixed = jnp.sum(mix_weights[:, :, None] * picked, axis=1)
    return mixed.astype(jnp.bfloat16)


MESH = pl.DeviceIdType.MESH
F32 = jnp.float32
BF16 = jnp.bfloat16
NZ, NX = 4, 2
UNITS = NZ * NX


def mesh_xor(z, d):
    high = lax.rem(lax.div(z, 2) + lax.div(d, 2), 2)
    low = lax.rem(lax.rem(z, 2) + lax.rem(d, 2), 2)
    return high * 2 + low


def dense_kernel(
    tokens, route, gate, up, down, out,
    got, upv, downv, wt, core_out, core_in, kept, y_out, y_in, hid, acc, x_out, x_in, z_out, z_in,
    tok_s, tok_r, w_s, w_r, core_s, core_r, y_s, y_r, hid_s, hid_r, x_s, x_r, z_s, z_r, load,
):
    expert = lax.axis_index("expert")
    part = lax.axis_index("dp")
    z, x = lax.div(expert, NX), lax.rem(expert, NX)
    y, core = lax.div(part, 2), lax.rem(part, 2)
    half = upv.shape[2]
    rows = tokens.shape[0]

    def at(d, other):
        xx = 1 - x if other else x
        return {"expert": mesh_xor(z, d) * NX + xx}

    x_peer = {"expert": z * NX + 1 - x}
    core_peer = {"dp": y * 2 + 1 - core}
    y_peer = {"dp": (1 - y) * 2 + core}

    def remote(src, dst, send, recv, device):
        return pltpu.make_async_remote_copy(
            src_ref=src, dst_ref=dst, send_sem=send, recv_sem=recv,
            device_id=device, device_id_type=MESH,
        )

    def tok_z(d):
        return remote(tokens, got.at[2 * d], tok_s.at[2 * d], tok_r.at[2 * d], at(d, False))

    def tok_x(d):
        return remote(got.at[2 * d], got.at[2 * d + 1], tok_s.at[2 * d + 1], tok_r.at[2 * d + 1], x_peer)

    def own_x():
        return remote(tokens, got.at[1], tok_s.at[1], tok_r.at[1], x_peer)

    def weight(k):
        return remote(wt.at[0], wt.at[k], w_s.at[k], w_r.at[k], at(k // 2, k % 2 == 1))

    def weight_in(u):
        return remote(wt.at[0], wt.at[u], w_s.at[u], w_r.at[u], x_peer)

    def core_copy(u):
        return remote(core_out.at[u], core_in.at[u], core_s.at[u], core_r.at[u], core_peer)

    def y_copy(u):
        return remote(y_out.at[u], y_in.at[u], y_s.at[u], y_r.at[u], y_peer)

    def hid_copy(u):
        return remote(hid.at[u, 0], hid.at[u, 1], hid_s.at[u], hid_r.at[u], core_peer)

    def x_copy(d):
        return remote(x_out.at[d], x_in.at[d], x_s.at[d], x_r.at[d], x_peer)

    def z_copy(d):
        return remote(z_out.at[d], z_in.at[d], z_s.at[d], z_r.at[d], at(d, False))

    own = pl.ds(pl.multiple_of(core * half, half), half)
    theirs = pl.ds(pl.multiple_of((1 - core) * half, half), half)
    loads = [
        pltpu.make_async_copy(tokens, got.at[0], load.at[0]),
        pltpu.make_async_copy(up.at[0, :, theirs], upv.at[1], load.at[1]),
        pltpu.make_async_copy(up.at[0, :, own], upv.at[0], load.at[2]),
        pltpu.make_async_copy(down.at[0, own, :], downv.at[0], load.at[3]),
        pltpu.make_async_copy(down.at[0, theirs, :], downv.at[1], load.at[4]),
    ]
    for copy in loads:
        copy.start()

    barrier = pltpu.get_barrier_semaphore()
    peers = [at(k // 2, k % 2 == 1) for k in range(1, UNITS)] + [core_peer, y_peer]
    for peer in peers:
        pl.semaphore_signal(barrier, inc=1, device_id=peer, device_id_type=MESH)
    pl.semaphore_wait(barrier, len(peers))

    own_x().start()
    for d in range(1, NZ):
        tok_z(d).start()

    scores = gate[...]
    mix = scores * (ROUTE_SCALE / jnp.sum(scores, axis=1, keepdims=True))
    ids = route[...]
    lanes = lax.broadcasted_iota(jnp.int32, (rows, 128), 1)
    spread = jnp.zeros((rows, 128), F32)
    for k in range(ids.shape[1]):
        spread = spread + jnp.where(ids[:, k:k + 1] == lanes, mix[:, k:k + 1], 0.0)
    wt[0] = spread.T[:UNITS, :]
    for k in range(1, UNITS):
        weight(k).start()
    for copy in loads:
        copy.wait()

    def stage_a(u):
        @pl.when(u >= 1)
        def _():
            remote(tokens, got.at[u], tok_s.at[u], tok_r.at[u], x_peer).wait_recv()

        @pl.when((u >= 2) & (lax.rem(u, 2) == 0))
        def _():
            tok_x(lax.div(u, 2)).start()

        block = got[u]
        core_out[u] = jnp.dot(block, upv[1], preferred_element_type=F32).astype(BF16)
        core_copy(u).start()
        kept[u] = jnp.dot(block, upv[0], preferred_element_type=F32)

    def stage_b(u):
        core_copy(u).wait_recv()
        total = kept[u] + core_in[u].astype(F32)
        kept[u] = total
        y_out[u] = total.astype(BF16)
        y_copy(u).start()

    def stage_c(u):
        y_copy(u).wait_recv()
        before = kept[u] + y_in[u].astype(F32)
        hid[u, 0] = (before / (1.0 + jnp.exp(-before))).astype(BF16)
        hid_copy(u).start()

    def stage_d(u):
        @pl.when(u >= 1)
        def _():
            weight_in(u).wait_recv()

        scale = jnp.broadcast_to(wt[u, pl.ds(expert, 1), :], (128, rows)).T
        hid_copy(u).wait_recv()
        result = jnp.dot(hid[u, 0], downv[0], preferred_element_type=F32)
        result = result + jnp.dot(hid[u, 1], downv[1], preferred_element_type=F32)
        d = lax.div(u, 2)
        result = result * jnp.concatenate([scale] * (result.shape[1] // 128), axis=1)

        @pl.when(lax.rem(u, 2) == 0)
        def _():
            acc[d] = result

        @pl.when(lax.rem(u, 2) == 1)
        def _():
            x_out[d] = result.astype(BF16)
            x_copy(d).start()

    def stage_e(d):
        x_copy(d).wait_recv()
        total = acc[d] + x_in[d].astype(F32)

        @pl.when(d == 0)
        def _():
            acc[d] = total

        @pl.when(d > 0)
        def _():
            z_out[d] = total.astype(BF16)
            z_copy(d).start()

    def step(t, carry):
        @pl.when(t < UNITS)
        def _():
            stage_a(t)

        @pl.when((t >= 1) & (t < UNITS + 1))
        def _():
            stage_b(t - 1)

        @pl.when((t >= 2) & (t < UNITS + 2))
        def _():
            stage_c(t - 2)

        @pl.when((t >= 3) & (t < UNITS + 3))
        def _():
            stage_d(t - 3)

        @pl.when((t >= 5) & (lax.rem(t, 2) == 1))
        def _():
            stage_e(lax.div(t - 5, 2))

        return carry

    lax.fori_loop(0, UNITS + 4, step, 0)

    total = acc[0]
    for d in range(1, NZ):
        z_copy(d).wait_recv()
        total = total + z_in[d].astype(F32)
    out[...] = total.astype(BF16)

    own_x().wait_send()
    for d in range(1, NZ):
        tok_z(d).wait_send()
        tok_x(d).wait_send()
        z_copy(d).wait_send()
    for d in range(NZ):
        x_copy(d).wait_send()
    for u in range(UNITS):
        if u:
            weight(u).wait_send()
        core_copy(u).wait_send()
        y_copy(u).wait_send()
        hid_copy(u).wait_send()


def dense(tokens, route_ids, gate_scores, up_weight, down_weight):
    rows, features = tokens.shape
    hidden = up_weight.shape[2]
    half = hidden // 2
    vmem = pl.BlockSpec(memory_space=pltpu.VMEM)
    anywhere = pl.BlockSpec(memory_space=pl.ANY)
    dma = pltpu.SemaphoreType.DMA
    return pl.pallas_call(
        dense_kernel,
        out_shape=jax.ShapeDtypeStruct((rows, features), BF16),
        in_specs=[anywhere, vmem, vmem, anywhere, anywhere],
        out_specs=vmem,
        scratch_shapes=[
            pltpu.VMEM((UNITS, rows, features), BF16),
            pltpu.VMEM((2, features, half), BF16),
            pltpu.VMEM((2, half, features), BF16),
            pltpu.VMEM((UNITS, UNITS, rows), F32),
            pltpu.VMEM((UNITS, rows, half), BF16),
            pltpu.VMEM((UNITS, rows, half), BF16),
            pltpu.VMEM((UNITS, rows, half), F32),
            pltpu.VMEM((UNITS, rows, half), BF16),
            pltpu.VMEM((UNITS, rows, half), BF16),
            pltpu.VMEM((UNITS, 2, rows, half), BF16),
            pltpu.VMEM((NZ, rows, features), F32),
            pltpu.VMEM((NZ, rows, features), BF16),
            pltpu.VMEM((NZ, rows, features), BF16),
            pltpu.VMEM((NZ, rows, features), BF16),
            pltpu.VMEM((NZ, rows, features), BF16),
        ] + [dma((UNITS,))] * 10 + [dma((NZ,))] * 4 + [dma((5,))],
        compiler_params=pltpu.CompilerParams(
            collective_id=0, has_side_effects=True, vmem_limit_bytes=40 * 2**20
        ),
        cost_estimate=pl.CostEstimate(
            flops=4 * UNITS * rows * features * hidden,
            bytes_accessed=4 * features * hidden + 4 * rows * features,
            transcendentals=UNITS * rows * half,
        ),
    )(tokens, route_ids, gate_scores, up_weight, down_weight)


def local(tokens, route_ids, gate_scores, up_weight, down_weight):
    experts = lax.axis_size("expert")
    every = route_ids.shape[1] == experts == UNITS and lax.axis_size("dp") == 4
    body = dense if every and tokens.shape[0] == 128 else routed
    return body(tokens, route_ids, gate_scores, up_weight, down_weight)


def solution(mesh):
    return jax.shard_map(
        local,
        mesh=mesh,
        in_specs=(
            P("expert", "dp"),
            P("expert", None),
            P("expert", None),
            P("expert", "dp", None),
            P("expert", None, "dp"),
        ),
        out_specs=P("expert", "dp"),
        check_vma=False,
    )
```

```python
import functools

import jax
import jax.numpy as jnp
from jax import lax
from jax.experimental import pallas as pl
from jax.experimental.pallas import tpu as pltpu
from jax.sharding import PartitionSpec as P

HOT = 2


ROUTE_SCALE = 2.5


def silu_hidden(before):
    summed = lax.psum(before.astype(jnp.bfloat16), "dp").astype(jnp.float32)
    result = jax.nn.silu(summed).astype(jnp.bfloat16)
    return result


def routed(tokens, route_ids, gate_scores, up_weight, down_weight):
    token_count, chosen_count = route_ids.shape
    features = tokens.shape[1]
    experts = lax.axis_size("expert")
    mean_rows = token_count * chosen_count // experts
    hot_most = min(2 * mean_rows - 1, token_count)
    cold_rows = (experts - HOT) * mean_rows - HOT * (hot_most - mean_rows)
    cold_most = -(-cold_rows // (experts - HOT))
    flat_ids = route_ids.reshape(-1)
    row_total = flat_ids.shape[0]
    expert_range = jnp.arange(experts, dtype=jnp.int32)
    onehot = (flat_ids[:, None] == expert_range[None, :]).astype(jnp.int32)
    running = jnp.cumsum(onehot, axis=0) - 1
    row_ranks = jnp.sum(onehot * running, axis=1)
    padded = jnp.concatenate([tokens, jnp.zeros((1, features), tokens.dtype)], axis=0)
    up_local = up_weight[0]
    down_local = down_weight[0]
    mix_weights = gate_scores * (ROUTE_SCALE / jnp.sum(gate_scores, axis=1, keepdims=True))
    slot_count = max(hot_most, cold_most)
    slot_of_row = flat_ids * slot_count + row_ranks
    slot_table = jnp.full((experts * slot_count,), row_total, jnp.int32)
    slot_table = slot_table.at[slot_of_row].set(jnp.arange(row_total, dtype=jnp.int32), mode="drop")
    sending = padded[slot_table // chosen_count].reshape(experts, slot_count, features)
    arrived = lax.all_to_all(sending, "expert", split_axis=0, concat_axis=0, tiled=True)
    item_count = arrived.shape[1]
    flat_rows = arrived.reshape(-1, features)
    before = jnp.dot(flat_rows, up_local, preferred_element_type=jnp.float32)
    hidden = silu_hidden(before)
    output = jnp.dot(hidden, down_local, preferred_element_type=jnp.float32)
    outcome = output.astype(jnp.bfloat16).reshape(experts, item_count, features)
    returned = lax.all_to_all(outcome, "expert", split_axis=0, concat_axis=0, tiled=True).reshape(
        -1, features
    )
    picked = returned[slot_of_row]
    picked = picked.reshape(token_count, chosen_count, features).astype(jnp.float32)
    mixed = jnp.sum(mix_weights[:, :, None] * picked, axis=1)
    return mixed.astype(jnp.bfloat16)


MESH = pl.DeviceIdType.MESH
F32 = jnp.float32
BF16 = jnp.bfloat16
NZ, NX = 4, 2
UNITS = NZ * NX


def mesh_xor(z, d):
    high = lax.rem(lax.div(z, 2) + lax.div(d, 2), 2)
    low = lax.rem(lax.rem(z, 2) + lax.rem(d, 2), 2)
    return high * 2 + low


def dense_kernel(
    tokens, route, gate, up, down, out,
    got, upv, downv, wt, core_out, core_in, kept, y_out, y_in, hid, acc, over, x_out, x_in, z_out, z_in,
    tok_s, tok_r, w_s, w_r, core_s, core_r, y_s, y_r, hid_s, hid_r, x_s, x_r, z_s, z_r, load,
):
    expert = lax.axis_index("expert")
    part = lax.axis_index("dp")
    z, x = lax.div(expert, NX), lax.rem(expert, NX)
    y, core = lax.div(part, 2), lax.rem(part, 2)
    half = upv.shape[2]
    rows = tokens.shape[0]

    def at(d, other):
        xx = 1 - x if other else x
        return {"expert": mesh_xor(z, d) * NX + xx}

    x_peer = {"expert": z * NX + 1 - x}
    core_peer = {"dp": y * 2 + 1 - core}
    y_peer = {"dp": (1 - y) * 2 + core}

    def remote(src, dst, send, recv, device):
        return pltpu.make_async_remote_copy(
            src_ref=src, dst_ref=dst, send_sem=send, recv_sem=recv,
            device_id=device, device_id_type=MESH,
        )

    inner = lax.rem(mesh_xor(z, lax.div(z, 2)), 2)
    is_inner = inner == 1
    near, across = at(1, False), at(3, False)

    def token(k, src, slot, device):
        return remote(src, got.at[slot], tok_s.at[k], tok_r.at[slot], device)

    def token_in(u):
        return remote(tokens, got.at[u], tok_s.at[0], tok_r.at[u], x_peer)

    own_x = token(0, tokens, 1, x_peer)
    own_near = token(1, tokens, 2, near)
    own_across = token(2, tokens, 6, across)
    near_across = token(3, got.at[2], 4, across)
    side_near = token(4, got.at[1], 3, near)
    across_near = token(5, got.at[6], 4, near)
    far_near = token(6, got.at[4], 6, near)
    middle_x = token(7, got.at[4], 5, x_peer)
    last_x = token(8, got.at[6], 7, x_peer)

    def weight(k):
        return remote(wt.at[0], wt.at[k], w_s.at[k], w_r.at[k], at(k // 2, k % 2 == 1))

    def weight_in(u):
        return remote(wt.at[0], wt.at[u], w_s.at[u], w_r.at[u], x_peer)

    def core_copy(u):
        return remote(core_out.at[u], core_in.at[u], core_s.at[u], core_r.at[u], core_peer)

    def y_copy(u):
        return remote(y_out.at[u], y_in.at[u], y_s.at[u], y_r.at[u], y_peer)

    def hid_copy(u):
        return remote(hid.at[u, 0], hid.at[u, 1], hid_s.at[u], hid_r.at[u], core_peer)

    def x_copy(d):
        return remote(x_out.at[d], x_in.at[d], x_s.at[d], x_r.at[d], x_peer)

    def over_copy():
        return remote(over.at[1], over.at[2], z_s.at[0], z_r.at[0], near)

    def z_copy(d):
        return remote(z_out.at[d], z_in.at[d], z_s.at[d], z_r.at[d], at(d, False))

    own = pl.ds(pl.multiple_of(core * half, half), half)
    theirs = pl.ds(pl.multiple_of((1 - core) * half, half), half)
    loads = [
        pltpu.make_async_copy(tokens, got.at[0], load.at[0]),
        pltpu.make_async_copy(up.at[0, :, theirs], upv.at[1], load.at[1]),
        pltpu.make_async_copy(up.at[0, :, own], upv.at[0], load.at[2]),
        pltpu.make_async_copy(down.at[0, own, :], downv.at[0], load.at[3]),
        pltpu.make_async_copy(down.at[0, theirs, :], downv.at[1], load.at[4]),
    ]
    for copy in loads:
        copy.start()

    barrier = pltpu.get_barrier_semaphore()
    peers = [at(k // 2, k % 2 == 1) for k in range(1, UNITS)] + [core_peer, y_peer]
    for peer in peers:
        pl.semaphore_signal(barrier, inc=1, device_id=peer, device_id_type=MESH)
    pl.semaphore_wait(barrier, len(peers))

    own_x.start()
    own_near.start()

    @pl.when(is_inner)
    def _():
        own_across.start()

    scores = gate[...]
    mix = scores * (ROUTE_SCALE / jnp.sum(scores, axis=0, keepdims=True))
    ids = route[...]
    named = lax.broadcasted_iota(jnp.int32, (UNITS, rows), 0)
    spread = jnp.zeros((UNITS, rows), F32)
    for k in range(UNITS):
        spread = spread + jnp.where(ids[k:k + 1, :] == named, mix[k:k + 1, :], 0.0)
    wt[0] = spread
    for k in range(1, UNITS):
        weight(k).start()
    for copy in loads:
        copy.wait()

    def stage_a(u):
        @pl.when(u > 0)
        def _():
            token_in(u).wait_recv()

        @pl.when(u == 1)
        def _():
            side_near.start()

        @pl.when((u == 2) & is_inner)
        def _():
            near_across.start()

        @pl.when(u == 4)
        def _():
            middle_x.start()

        @pl.when(u == 6)
        def _():
            last_x.start()

        @pl.when((u == 4) & is_inner)
        def _():
            far_near.start()

        @pl.when((u == 6) & is_inner)
        def _():
            across_near.start()

        block = got[u]
        core_out[u] = jnp.dot(block, upv[1], preferred_element_type=F32).astype(BF16)
        core_copy(u).start()
        kept[u] = jnp.dot(block, upv[0], preferred_element_type=F32)

    def stage_b(u):
        core_copy(u).wait_recv()
        total = kept[u] + core_in[u].astype(F32)
        kept[u] = total
        y_out[u] = total.astype(BF16)
        y_copy(u).start()

    def stage_c(u):
        y_copy(u).wait_recv()
        before = kept[u] + y_in[u].astype(F32)
        hid[u, 0] = (before / (1.0 + jnp.exp(-before))).astype(BF16)
        hid_copy(u).start()

    def stage_d(u):
        @pl.when(u >= 1)
        def _():
            weight_in(u).wait_recv()

        scale = jnp.broadcast_to(wt[u, pl.ds(expert, 1), :], (128, rows)).T
        hid_copy(u).wait_recv()
        result = jnp.dot(hid[u, 0], downv[0], preferred_element_type=F32)
        result = result + jnp.dot(hid[u, 1], downv[1], preferred_element_type=F32)
        d = lax.div(u, 2)
        result = result * jnp.concatenate([scale] * (result.shape[1] // 128), axis=1)

        @pl.when((lax.rem(u, 2) == 0) & (u != 2))
        def _():
            acc[d] = result

        @pl.when(u == 2)
        def _():
            z_out[1] = result.astype(BF16)
            z_copy(1).start()

        @pl.when(u == 1)
        def _():
            over[0] = result.astype(BF16)

        @pl.when(u == 3)
        def _():
            over[1] = result.astype(BF16)
            over_copy().start()

        @pl.when((u == 5) | (u == 7))
        def _():
            x_out[d] = result.astype(BF16)
            x_copy(d).start()

    def stage_e(d):
        x_copy(d).wait_recv()
        z_out[d] = (acc[d] + x_in[d].astype(F32)).astype(BF16)
        z_copy(d).start()

    outer_order, inner_order = [0, 2, 1, 4, 5, 6, 3, 7], [0, 2, 1, 6, 7, 4, 3, 5]
    packed = [sum(v << (3 * k) for k, v in enumerate(o)) for o in (outer_order, inner_order)]
    order = packed[0] + inner * (packed[1] - packed[0])

    def slot(k):
        return lax.rem(lax.shift_right_logical(order, 3 * k), UNITS)

    def step(t, carry):
        @pl.when(t < UNITS)
        def _():
            stage_a(slot(t))

        @pl.when((t >= 1) & (t < UNITS + 1))
        def _():
            stage_b(slot(t - 1))

        @pl.when((t >= 2) & (t < UNITS + 2))
        def _():
            stage_c(slot(t - 2))

        @pl.when((t >= 3) & (t < UNITS + 3))
        def _():
            stage_d(slot(t - 3))

        @pl.when(t == 9)
        def _():
            stage_e(lax.div(slot(3), 2))

        return carry

    lax.fori_loop(0, UNITS + 3, step, 0)

    over_copy().wait_recv()
    x_out[0] = (over[0].astype(F32) + over[2].astype(F32)).astype(BF16)
    x_copy(0).start()
    stage_e(lax.div(slot(7), 2))

    x_copy(0).wait_recv()
    total = acc[0] + x_in[0].astype(F32)
    for d in range(1, NZ):
        z_copy(d).wait_recv()
        total = total + z_in[d].astype(F32)
    out[...] = total.astype(BF16)

    for copy in (own_x, own_near, side_near, middle_x, last_x, over_copy()):
        copy.wait_send()

    @pl.when(is_inner)
    def _():
        for copy in (own_across, near_across, far_near, across_near):
            copy.wait_send()

    for d in range(NZ):
        if d:
            z_copy(d).wait_send()
        if d != 1:
            x_copy(d).wait_send()
    for u in range(UNITS):
        if u:
            weight(u).wait_send()
        core_copy(u).wait_send()
        y_copy(u).wait_send()
        hid_copy(u).wait_send()


def dense(tokens, route_ids, gate_scores, up_weight, down_weight):
    rows, features = tokens.shape
    hidden = up_weight.shape[2]
    half = hidden // 2
    vmem = pl.BlockSpec(memory_space=pltpu.VMEM)
    anywhere = pl.BlockSpec(memory_space=pl.ANY)
    dma = pltpu.SemaphoreType.DMA
    return pl.pallas_call(
        dense_kernel,
        out_shape=jax.ShapeDtypeStruct((rows, features), BF16),
        in_specs=[anywhere, vmem, vmem, anywhere, anywhere],
        out_specs=vmem,
        scratch_shapes=[
            pltpu.VMEM((UNITS, rows, features), BF16),
            pltpu.VMEM((2, features, half), BF16),
            pltpu.VMEM((2, half, features), BF16),
            pltpu.VMEM((UNITS, UNITS, rows), F32),
            pltpu.VMEM((UNITS, rows, half), BF16),
            pltpu.VMEM((UNITS, rows, half), BF16),
            pltpu.VMEM((UNITS, rows, half), F32),
            pltpu.VMEM((UNITS, rows, half), BF16),
            pltpu.VMEM((UNITS, rows, half), BF16),
            pltpu.VMEM((UNITS, 2, rows, half), BF16),
            pltpu.VMEM((NZ, rows, features), F32),
            pltpu.VMEM((3, rows, features), BF16),
            pltpu.VMEM((NZ, rows, features), BF16),
            pltpu.VMEM((NZ, rows, features), BF16),
            pltpu.VMEM((NZ, rows, features), BF16),
            pltpu.VMEM((NZ, rows, features), BF16),
        ] + [dma((9,))] + [dma((UNITS,))] * 9 + [dma((NZ,))] * 4 + [dma((5,))],
        compiler_params=pltpu.CompilerParams(
            collective_id=0, has_side_effects=True, vmem_limit_bytes=63 * 2**20
        ),
        cost_estimate=pl.CostEstimate(
            flops=4 * UNITS * rows * features * hidden,
            bytes_accessed=4 * features * hidden + 4 * rows * features,
            transcendentals=UNITS * rows * half,
        ),
    )(tokens, route_ids.T, gate_scores.T, up_weight, down_weight)


def local(tokens, route_ids, gate_scores, up_weight, down_weight):
    experts = lax.axis_size("expert")
    every = route_ids.shape[1] == experts == UNITS and lax.axis_size("dp") == 4
    body = dense if every and tokens.shape[0] == 128 else routed
    return body(tokens, route_ids, gate_scores, up_weight, down_weight)


def solution(mesh):
    return jax.shard_map(
        local,
        mesh=mesh,
        in_specs=(
            P("expert", "dp"),
            P("expert", None),
            P("expert", None),
            P("expert", "dp", None),
            P("expert", None, "dp"),
        ),
        out_specs=P("expert", "dp"),
        check_vma=False,
    )
```

```python
import functools

import jax
import jax.numpy as jnp
from jax import lax
from jax.experimental import pallas as pl
from jax.experimental.pallas import tpu as pltpu
from jax.sharding import PartitionSpec as P

HOT = 2


ROUTE_SCALE = 2.5


def silu_hidden(before):
    summed = lax.psum(before.astype(jnp.bfloat16), "dp").astype(jnp.float32)
    result = jax.nn.silu(summed).astype(jnp.bfloat16)
    return result


def routed(tokens, route_ids, gate_scores, up_weight, down_weight):
    token_count, chosen_count = route_ids.shape
    features = tokens.shape[1]
    experts = lax.axis_size("expert")
    mean_rows = token_count * chosen_count // experts
    hot_most = min(2 * mean_rows - 1, token_count)
    cold_rows = (experts - HOT) * mean_rows - HOT * (hot_most - mean_rows)
    cold_most = -(-cold_rows // (experts - HOT))
    flat_ids = route_ids.reshape(-1)
    row_total = flat_ids.shape[0]
    expert_range = jnp.arange(experts, dtype=jnp.int32)
    onehot = (flat_ids[:, None] == expert_range[None, :]).astype(jnp.int32)
    running = jnp.cumsum(onehot, axis=0) - 1
    row_ranks = jnp.sum(onehot * running, axis=1)
    padded = jnp.concatenate([tokens, jnp.zeros((1, features), tokens.dtype)], axis=0)
    up_local = up_weight[0]
    down_local = down_weight[0]
    mix_weights = gate_scores * (ROUTE_SCALE / jnp.sum(gate_scores, axis=1, keepdims=True))
    slot_count = max(hot_most, cold_most)
    slot_of_row = flat_ids * slot_count + row_ranks
    slot_table = jnp.full((experts * slot_count,), row_total, jnp.int32)
    slot_table = slot_table.at[slot_of_row].set(jnp.arange(row_total, dtype=jnp.int32), mode="drop")
    sending = padded[slot_table // chosen_count].reshape(experts, slot_count, features)
    arrived = lax.all_to_all(sending, "expert", split_axis=0, concat_axis=0, tiled=True)
    item_count = arrived.shape[1]
    flat_rows = arrived.reshape(-1, features)
    before = jnp.dot(flat_rows, up_local, preferred_element_type=jnp.float32)
    hidden = silu_hidden(before)
    output = jnp.dot(hidden, down_local, preferred_element_type=jnp.float32)
    outcome = output.astype(jnp.bfloat16).reshape(experts, item_count, features)
    returned = lax.all_to_all(outcome, "expert", split_axis=0, concat_axis=0, tiled=True).reshape(
        -1, features
    )
    picked = returned[slot_of_row]
    picked = picked.reshape(token_count, chosen_count, features).astype(jnp.float32)
    mixed = jnp.sum(mix_weights[:, :, None] * picked, axis=1)
    return mixed.astype(jnp.bfloat16)


MESH = pl.DeviceIdType.MESH
F32 = jnp.float32
BF16 = jnp.bfloat16
NZ, NX = 4, 2
UNITS = NZ * NX


def mesh_xor(z, d):
    high = lax.rem(lax.div(z, 2) + lax.div(d, 2), 2)
    low = lax.rem(lax.rem(z, 2) + lax.rem(d, 2), 2)
    return high * 2 + low


def dense_kernel(
    tokens, route, gate, up, down, out,
    got, upv, downv, wt, core_out, core_in, kept, y_out, y_in, hid, acc, over, x_out, x_in, z_out, z_in,
    tok_s, tok_r, w_s, w_r, core_s, core_r, y_s, y_r, hid_s, hid_r, x_s, x_r, z_s, z_r, load,
):
    expert = lax.axis_index("expert")
    part = lax.axis_index("dp")
    z, x = lax.div(expert, NX), lax.rem(expert, NX)
    y, core = lax.div(part, 2), lax.rem(part, 2)
    half = upv.shape[2]
    rows = tokens.shape[0]

    def at(d, other):
        xx = 1 - x if other else x
        return {"expert": mesh_xor(z, d) * NX + xx}

    x_peer = {"expert": z * NX + 1 - x}
    core_peer = {"dp": y * 2 + 1 - core}
    y_peer = {"dp": (1 - y) * 2 + core}

    def remote(src, dst, send, recv, device):
        return pltpu.make_async_remote_copy(
            src_ref=src, dst_ref=dst, send_sem=send, recv_sem=recv,
            device_id=device, device_id_type=MESH,
        )

    inner = lax.rem(mesh_xor(z, lax.div(z, 2)), 2)
    is_inner = inner == 1
    near, across = at(1, False), at(3, False)

    def token(k, src, slot, device):
        return remote(src, got.at[slot], tok_s.at[k], tok_r.at[slot], device)

    def token_in(u):
        return remote(tokens, got.at[u], tok_s.at[0], tok_r.at[u], x_peer)

    second, third = 2 + inner, 3 - inner
    own_x = token(0, tokens, 2, x_peer)
    own_near = token(1, tokens, 1, near)
    own_across = token(2, tokens, 3, across)
    near_across = token(3, got.at[1], 5, across)
    side_near = token(4, got.at[2], 6, near)
    across_near = token(5, got.at[3], 3, near)
    far_near = token(6, got.at[5], 5, near)
    second_x = token(7, got.at[3], 4, x_peer)
    third_x = token(8, got.at[5], 7, x_peer)

    def weight(k):
        return remote(wt.at[0], wt.at[k], w_s.at[k], w_r.at[k], at(k // 2, k % 2 == 1))

    def weight_in(u):
        return remote(wt.at[0], wt.at[u], w_s.at[u], w_r.at[u], x_peer)

    def core_copy(u):
        return remote(core_out.at[u], core_in.at[u], core_s.at[u], core_r.at[u], core_peer)

    def y_copy(u):
        return remote(y_out.at[u], y_in.at[u], y_s.at[u], y_r.at[u], y_peer)

    def hid_copy(u):
        return remote(hid.at[u, 0], hid.at[u, 1], hid_s.at[u], hid_r.at[u], core_peer)

    def x_copy(d):
        return remote(x_out.at[d], x_in.at[d], x_s.at[d], x_r.at[d], x_peer)

    def over_copy():
        return remote(over.at[1], over.at[2], z_s.at[0], z_r.at[0], near)

    def z_copy(d):
        return remote(z_out.at[d], z_in.at[d], z_s.at[d], z_r.at[d], at(d, False))

    own = pl.ds(pl.multiple_of(core * half, half), half)
    theirs = pl.ds(pl.multiple_of((1 - core) * half, half), half)
    loads = [
        pltpu.make_async_copy(tokens, got.at[0], load.at[0]),
        pltpu.make_async_copy(up.at[0, :, theirs], upv.at[1], load.at[1]),
        pltpu.make_async_copy(up.at[0, :, own], upv.at[0], load.at[2]),
        pltpu.make_async_copy(down.at[0, own, :], downv.at[0], load.at[3]),
        pltpu.make_async_copy(down.at[0, theirs, :], downv.at[1], load.at[4]),
    ]
    for copy in loads:
        copy.start()

    barrier = pltpu.get_barrier_semaphore()
    peers = [at(k // 2, k % 2 == 1) for k in range(1, UNITS)] + [core_peer, y_peer]
    for peer in peers:
        pl.semaphore_signal(barrier, inc=1, device_id=peer, device_id_type=MESH)
    pl.semaphore_wait(barrier, len(peers))

    own_x.start()
    own_near.start()

    @pl.when(is_inner)
    def _():
        own_across.start()

    scores = gate[...]
    mix = scores * (ROUTE_SCALE / jnp.sum(scores, axis=0, keepdims=True))
    ids = route[...]
    named = lax.broadcasted_iota(jnp.int32, (UNITS, rows), 0)
    spread = jnp.zeros((UNITS, rows), F32)
    for k in range(UNITS):
        spread = spread + jnp.where(ids[k:k + 1, :] == named, mix[k:k + 1, :], 0.0)
    wt[0] = spread
    for k in range(1, UNITS):
        weight(k).start()
    for copy in loads:
        copy.wait()

    def first_arrivals():
        token_in(1).wait_recv()

        @pl.when(is_inner)
        def _():
            near_across.start()
            token_in(3).wait_recv()
            across_near.start()
            second_x.start()

        token_in(2).wait_recv()

        @pl.when(jnp.logical_not(is_inner))
        def _():
            side_near.start()

    def second_arrivals():
        @pl.when(is_inner)
        def _():
            token_in(5).wait_recv()
            far_near.start()
            side_near.start()
            third_x.start()

        @pl.when(jnp.logical_not(is_inner))
        def _():
            token_in(3).wait_recv()
            second_x.start()

    def third_arrivals():
        @pl.when(jnp.logical_not(is_inner))
        def _():
            token_in(5).wait_recv()
            third_x.start()

        token_in(4).wait_recv()

    def stage_a(u):
        @pl.when(u >= 6)
        def _():
            token_in(u).wait_recv()

        block = got[u]
        core_out[u] = jnp.dot(block, upv[1], preferred_element_type=F32).astype(BF16)
        core_copy(u).start()
        kept[u] = jnp.dot(block, upv[0], preferred_element_type=F32)

    def stage_b(u):
        core_copy(u).wait_recv()
        total = kept[u] + core_in[u].astype(F32)
        kept[u] = total
        y_out[u] = total.astype(BF16)
        y_copy(u).start()

    def stage_c(u):
        y_copy(u).wait_recv()
        before = kept[u] + y_in[u].astype(F32)
        hid[u, 0] = (before / (1.0 + jnp.exp(-before))).astype(BF16)
        hid_copy(u).start()

    def stage_d(u):
        other = (u == 2) | (u == 4) | (u >= 6)
        d = jnp.where((u == 1) | (u == 6), 1, jnp.where((u == 3) | (u == 4), second, third))
        d = jnp.where((u == 0) | (u == 2), 0, d)
        k = 2 * d + other.astype(jnp.int32)

        @pl.when(u >= 1)
        def _():
            weight_in(k).wait_recv()

        scale = jnp.broadcast_to(wt[k, pl.ds(expert, 1), :], (128, rows)).T
        hid_copy(u).wait_recv()
        result = jnp.dot(hid[u, 0], downv[0], preferred_element_type=F32)
        result = result + jnp.dot(hid[u, 1], downv[1], preferred_element_type=F32)
        result = result * jnp.concatenate([scale] * (result.shape[1] // 128), axis=1)

        @pl.when((u == 0) | (u == 3) | (u == 5))
        def _():
            acc[d] = result

        @pl.when(u == 1)
        def _():
            z_out[1] = result.astype(BF16)
            z_copy(1).start()

        @pl.when(u == 2)
        def _():
            over[0] = result.astype(BF16)

        @pl.when(u == 6)
        def _():
            over[1] = result.astype(BF16)
            over_copy().start()

        @pl.when((u == 4) | (u == 7))
        def _():
            x_out[d] = result.astype(BF16)
            x_copy(d).start()

    def stage_e(d):
        x_copy(d).wait_recv()
        z_out[d] = (acc[d] + x_in[d].astype(F32)).astype(BF16)
        z_copy(d).start()

    def step(t, carry):
        @pl.when(t == 1)
        def _():
            first_arrivals()

        @pl.when(t == 3)
        def _():
            second_arrivals()

        @pl.when(t == 4)
        def _():
            third_arrivals()

        @pl.when(t < UNITS)
        def _():
            stage_a(t)

        @pl.when((t >= 1) & (t < UNITS + 1))
        def _():
            stage_b(t - 1)

        @pl.when((t >= 2) & (t < UNITS + 2))
        def _():
            stage_c(t - 2)

        @pl.when((t >= 3) & (t < UNITS + 3))
        def _():
            stage_d(t - 3)

        @pl.when(t == 8)
        def _():
            stage_e(second)

        return carry

    lax.fori_loop(0, UNITS + 3, step, 0)

    stage_e(third)
    over_copy().wait_recv()
    x_out[0] = (over[0].astype(F32) + over[2].astype(F32)).astype(BF16)
    x_copy(0).start()

    x_copy(0).wait_recv()
    total = acc[0] + x_in[0].astype(F32)
    for d in range(1, NZ):
        z_copy(d).wait_recv()
        total = total + z_in[d].astype(F32)
    out[...] = total.astype(BF16)

    for copy in (own_x, own_near, side_near, second_x, third_x, over_copy()):
        copy.wait_send()

    @pl.when(is_inner)
    def _():
        for copy in (own_across, near_across, far_near, across_near):
            copy.wait_send()

    for d in range(NZ):
        if d:
            z_copy(d).wait_send()
        if d != 1:
            x_copy(d).wait_send()
    for u in range(UNITS):
        if u:
            weight(u).wait_send()
        core_copy(u).wait_send()
        y_copy(u).wait_send()
        hid_copy(u).wait_send()


def dense(tokens, route_ids, gate_scores, up_weight, down_weight):
    rows, features = tokens.shape
    hidden = up_weight.shape[2]
    half = hidden // 2
    vmem = pl.BlockSpec(memory_space=pltpu.VMEM)
    hbm = pl.BlockSpec(memory_space=pltpu.HBM)
    dma = pltpu.SemaphoreType.DMA
    return pl.pallas_call(
        dense_kernel,
        out_shape=jax.ShapeDtypeStruct((rows, features), BF16),
        in_specs=[hbm, vmem, vmem, hbm, hbm],
        out_specs=vmem,
        scratch_shapes=[
            pltpu.VMEM((UNITS, rows, features), BF16),
            pltpu.VMEM((2, features, half), BF16),
            pltpu.VMEM((2, half, features), BF16),
            pltpu.VMEM((UNITS, UNITS, rows), F32),
            pltpu.VMEM((UNITS, rows, half), BF16),
            pltpu.VMEM((UNITS, rows, half), BF16),
            pltpu.VMEM((UNITS, rows, half), F32),
            pltpu.VMEM((UNITS, rows, half), BF16),
            pltpu.VMEM((UNITS, rows, half), BF16),
            pltpu.VMEM((UNITS, 2, rows, half), BF16),
            pltpu.VMEM((NZ, rows, features), F32),
            pltpu.VMEM((3, rows, features), BF16),
            pltpu.VMEM((NZ, rows, features), BF16),
            pltpu.VMEM((NZ, rows, features), BF16),
            pltpu.VMEM((NZ, rows, features), BF16),
            pltpu.VMEM((NZ, rows, features), BF16),
        ] + [dma((9,))] + [dma((UNITS,))] * 9 + [dma((NZ,))] * 4 + [dma((5,))],
        compiler_params=pltpu.CompilerParams(
            collective_id=0, has_side_effects=True, vmem_limit_bytes=63 * 2**20
        ),
        cost_estimate=pl.CostEstimate(
            flops=4 * UNITS * rows * features * hidden,
            bytes_accessed=4 * features * hidden + 4 * rows * features,
            transcendentals=UNITS * rows * half,
        ),
    )(tokens, route_ids.T, gate_scores.T, up_weight, down_weight)


def local(tokens, route_ids, gate_scores, up_weight, down_weight):
    experts = lax.axis_size("expert")
    every = route_ids.shape[1] == experts == UNITS and lax.axis_size("dp") == 4
    body = dense if every and tokens.shape[0] == 128 else routed
    return body(tokens, route_ids, gate_scores, up_weight, down_weight)


def solution(mesh):
    return jax.shard_map(
        local,
        mesh=mesh,
        in_specs=(
            P("expert", "dp"),
            P("expert", None),
            P("expert", None),
            P("expert", "dp", None),
            P("expert", None, "dp"),
        ),
        out_specs=P("expert", "dp"),
        check_vma=False,
    )
```

```python
import functools

import jax
import jax.numpy as jnp
from jax import lax
from jax.experimental import pallas as pl
from jax.experimental.pallas import tpu as pltpu
from jax.sharding import PartitionSpec as P

HOT = 2


ROUTE_SCALE = 2.5


def silu_hidden(before):
    summed = lax.psum(before.astype(jnp.bfloat16), "dp").astype(jnp.float32)
    result = jax.nn.silu(summed).astype(jnp.bfloat16)
    return result


def routed(tokens, route_ids, gate_scores, up_weight, down_weight):
    token_count, chosen_count = route_ids.shape
    features = tokens.shape[1]
    experts = lax.axis_size("expert")
    mean_rows = token_count * chosen_count // experts
    hot_most = min(2 * mean_rows - 1, token_count)
    cold_rows = (experts - HOT) * mean_rows - HOT * (hot_most - mean_rows)
    cold_most = -(-cold_rows // (experts - HOT))
    flat_ids = route_ids.reshape(-1)
    row_total = flat_ids.shape[0]
    expert_range = jnp.arange(experts, dtype=jnp.int32)
    onehot = (flat_ids[:, None] == expert_range[None, :]).astype(jnp.int32)
    running = jnp.cumsum(onehot, axis=0) - 1
    row_ranks = jnp.sum(onehot * running, axis=1)
    padded = jnp.concatenate([tokens, jnp.zeros((1, features), tokens.dtype)], axis=0)
    up_local = up_weight[0]
    down_local = down_weight[0]
    mix_weights = gate_scores * (ROUTE_SCALE / jnp.sum(gate_scores, axis=1, keepdims=True))
    slot_count = max(hot_most, cold_most)
    slot_of_row = flat_ids * slot_count + row_ranks
    slot_table = jnp.full((experts * slot_count,), row_total, jnp.int32)
    slot_table = slot_table.at[slot_of_row].set(jnp.arange(row_total, dtype=jnp.int32), mode="drop")
    sending = padded[slot_table // chosen_count].reshape(experts, slot_count, features)
    arrived = lax.all_to_all(sending, "expert", split_axis=0, concat_axis=0, tiled=True)
    item_count = arrived.shape[1]
    flat_rows = arrived.reshape(-1, features)
    before = jnp.dot(flat_rows, up_local, preferred_element_type=jnp.float32)
    hidden = silu_hidden(before)
    output = jnp.dot(hidden, down_local, preferred_element_type=jnp.float32)
    outcome = output.astype(jnp.bfloat16).reshape(experts, item_count, features)
    returned = lax.all_to_all(outcome, "expert", split_axis=0, concat_axis=0, tiled=True).reshape(
        -1, features
    )
    picked = returned[slot_of_row]
    picked = picked.reshape(token_count, chosen_count, features).astype(jnp.float32)
    mixed = jnp.sum(mix_weights[:, :, None] * picked, axis=1)
    return mixed.astype(jnp.bfloat16)


MESH = pl.DeviceIdType.MESH
F32 = jnp.float32
BF16 = jnp.bfloat16
NZ, NX = 4, 2
UNITS = NZ * NX


def mesh_xor(z, d):
    high = lax.rem(lax.div(z, 2) + lax.div(d, 2), 2)
    low = lax.rem(lax.rem(z, 2) + lax.rem(d, 2), 2)
    return high * 2 + low


def dense_kernel(
    tokens, route, gate, up, down, out,
    got, upv, downv, wt, core_out, core_in, kept, y_out, y_in, hid, acc, over, x_out, x_in, z_out, z_in,
    tok_s, tok_r, w_s, w_r, core_s, core_r, y_s, y_r, hid_s, hid_r, x_s, x_r, z_s, z_r, load,
):
    expert = lax.axis_index("expert")
    part = lax.axis_index("dp")
    z, x = lax.div(expert, NX), lax.rem(expert, NX)
    y, core = lax.div(part, 2), lax.rem(part, 2)
    half = upv.shape[2]
    rows = tokens.shape[0]

    def at(d, other):
        xx = 1 - x if other else x
        return {"expert": mesh_xor(z, d) * NX + xx}

    x_peer = {"expert": z * NX + 1 - x}
    core_peer = {"dp": y * 2 + 1 - core}
    y_peer = {"dp": (1 - y) * 2 + core}

    def remote(src, dst, send, recv, device):
        return pltpu.make_async_remote_copy(
            src_ref=src, dst_ref=dst, send_sem=send, recv_sem=recv,
            device_id=device, device_id_type=MESH,
        )

    inner = lax.rem(mesh_xor(z, lax.div(z, 2)), 2)
    is_inner = inner == 1
    near, across = at(1, False), at(3, False)

    part_rows = rows // 2

    def token(k, src, slot, device):
        def piece(p):
            lines = pl.ds(p * part_rows, part_rows)
            return remote(src.at[lines], got.at[slot, lines], tok_s.at[k, p], tok_r.at[slot, p], device)
        return piece

    def token_in(u, p):
        lines = pl.ds(p * part_rows, part_rows)
        return remote(tokens.at[lines], got.at[u, lines], tok_s.at[0, p], tok_r.at[u, p], x_peer)

    second, third = 2 + inner, 3 - inner
    own_x = token(0, tokens, 2, x_peer)
    own_near = token(1, tokens, 1, near)
    own_across = token(2, tokens, 3, across)
    near_across = token(3, got.at[1], 5, across)
    side_near = token(4, got.at[2], 6, near)
    across_near = token(5, got.at[3], 3, near)
    far_near = token(6, got.at[5], 5, near)
    second_x = token(7, got.at[3], 4, x_peer)
    third_x = token(8, got.at[5], 7, x_peer)

    def weight(k):
        return remote(wt.at[0], wt.at[k], w_s.at[k], w_r.at[k], at(k // 2, k % 2 == 1))

    def weight_in(u):
        return remote(wt.at[0], wt.at[u], w_s.at[u], w_r.at[u], x_peer)

    def core_copy(u):
        return remote(core_out.at[u], core_in.at[u], core_s.at[u], core_r.at[u], core_peer)

    def y_copy(u):
        return remote(y_out.at[u], y_in.at[u], y_s.at[u], y_r.at[u], y_peer)

    def hid_copy(u):
        return remote(hid.at[u, 0], hid.at[u, 1], hid_s.at[u], hid_r.at[u], core_peer)

    def x_copy(d):
        return remote(x_out.at[d], x_in.at[d], x_s.at[d], x_r.at[d], x_peer)

    def over_copy():
        return remote(over.at[1], over.at[2], z_s.at[0], z_r.at[0], near)

    def z_copy(d):
        return remote(z_out.at[d], z_in.at[d], z_s.at[d], z_r.at[d], at(d, False))

    own = pl.ds(pl.multiple_of(core * half, half), half)
    theirs = pl.ds(pl.multiple_of((1 - core) * half, half), half)
    loads = [
        pltpu.make_async_copy(tokens, got.at[0], load.at[0]),
        pltpu.make_async_copy(up.at[0, :, theirs], upv.at[1], load.at[1]),
        pltpu.make_async_copy(up.at[0, :, own], upv.at[0], load.at[2]),
        pltpu.make_async_copy(down.at[0, own, :], downv.at[0], load.at[3]),
        pltpu.make_async_copy(down.at[0, theirs, :], downv.at[1], load.at[4]),
    ]
    for copy in loads:
        copy.start()

    barrier = pltpu.get_barrier_semaphore()
    peers = [at(k // 2, k % 2 == 1) for k in range(1, UNITS)] + [core_peer, y_peer]
    for peer in peers:
        pl.semaphore_signal(barrier, inc=1, device_id=peer, device_id_type=MESH)
    pl.semaphore_wait(barrier, len(peers))

    own_x(0).start()
    own_near(0).start()

    @pl.when(is_inner)
    def _():
        own_across(0).start()

    own_x(1).start()
    own_near(1).start()

    @pl.when(is_inner)
    def _():
        own_across(1).start()

    scores = gate[...]
    mix = scores * (ROUTE_SCALE / jnp.sum(scores, axis=0, keepdims=True))
    ids = route[...]
    named = lax.broadcasted_iota(jnp.int32, (UNITS, rows), 0)
    spread = jnp.zeros((UNITS, rows), F32)
    for k in range(UNITS):
        spread = spread + jnp.where(ids[k:k + 1, :] == named, mix[k:k + 1, :], 0.0)
    wt[0] = spread
    for k in range(1, UNITS):
        weight(k).start()
    for copy in loads:
        copy.wait()

    def first_arrivals():
        for p in range(2):
            token_in(1, p).wait_recv()

            @pl.when(is_inner)
            def _():
                near_across(p).start()
                token_in(3, p).wait_recv()
                across_near(p).start()
                second_x(p).start()

            token_in(2, p).wait_recv()

            @pl.when(jnp.logical_not(is_inner))
            def _():
                side_near(p).start()

    def second_arrivals():
        for p in range(2):
            @pl.when(is_inner)
            def _():
                token_in(5, p).wait_recv()
                far_near(p).start()
                third_x(p).start()

            @pl.when(jnp.logical_not(is_inner))
            def _():
                token_in(3, p).wait_recv()
                second_x(p).start()

        @pl.when(is_inner)
        def _():
            side_near(0).start()
            side_near(1).start()

    def third_arrivals():
        for p in range(2):
            @pl.when(jnp.logical_not(is_inner))
            def _():
                token_in(5, p).wait_recv()
                third_x(p).start()

        token_in(4, 0).wait_recv()
        token_in(4, 1).wait_recv()

    def stage_a(u):
        @pl.when(u >= 6)
        def _():
            token_in(u, 0).wait_recv()
            token_in(u, 1).wait_recv()

        block = got[u]
        core_out[u] = jnp.dot(block, upv[1], preferred_element_type=F32).astype(BF16)
        core_copy(u).start()
        kept[u] = jnp.dot(block, upv[0], preferred_element_type=F32)

    def stage_b(u):
        core_copy(u).wait_recv()
        total = kept[u] + core_in[u].astype(F32)
        kept[u] = total
        y_out[u] = total.astype(BF16)
        y_copy(u).start()

    def stage_c(u):
        y_copy(u).wait_recv()
        before = kept[u] + y_in[u].astype(F32)
        hid[u, 0] = (before / (1.0 + jnp.exp(-before))).astype(BF16)
        hid_copy(u).start()

    def stage_d(u):
        other = (u == 2) | (u == 4) | (u >= 6)
        d = jnp.where((u == 1) | (u == 6), 1, jnp.where((u == 3) | (u == 4), second, third))
        d = jnp.where((u == 0) | (u == 2), 0, d)
        k = 2 * d + other.astype(jnp.int32)

        @pl.when(u >= 1)
        def _():
            weight_in(k).wait_recv()

        scale = jnp.broadcast_to(wt[k, pl.ds(expert, 1), :], (128, rows)).T
        hid_copy(u).wait_recv()
        result = jnp.dot(hid[u, 0], downv[0], preferred_element_type=F32)
        result = result + jnp.dot(hid[u, 1], downv[1], preferred_element_type=F32)
        result = result * jnp.concatenate([scale] * (result.shape[1] // 128), axis=1)

        @pl.when((u == 0) | (u == 3) | (u == 5))
        def _():
            acc[d] = result

        @pl.when(u == 1)
        def _():
            z_out[1] = result.astype(BF16)

            @pl.when(jnp.logical_not(is_inner))
            def _():
                z_copy(1).start()

        @pl.when(u == 2)
        def _():
            over[0] = result.astype(BF16)

        @pl.when(u == 6)
        def _():
            over[1] = result.astype(BF16)
            over_copy().start()

        @pl.when((u == 4) | (u == 7))
        def _():
            x_out[d] = result.astype(BF16)
            x_copy(d).start()

    def stage_e(d):
        x_copy(d).wait_recv()
        z_out[d] = (acc[d] + x_in[d].astype(F32)).astype(BF16)
        z_copy(d).start()

    def step(t, carry):
        @pl.when((t >= 3) & (t < UNITS + 3))
        def _():
            stage_d(t - 3)

        @pl.when((t >= 2) & (t < UNITS + 2))
        def _():
            stage_c(t - 2)

        @pl.when((t >= 1) & (t < UNITS + 1))
        def _():
            stage_b(t - 1)

        @pl.when(t == 1)
        def _():
            first_arrivals()

        @pl.when(t == 3)
        def _():
            second_arrivals()

        @pl.when(t == 4)
        def _():
            third_arrivals()

        @pl.when((t == 7) & is_inner)
        def _():
            z_copy(1).start()

        @pl.when(t < UNITS)
        def _():
            stage_a(t)

        @pl.when(t == 8)
        def _():
            stage_e(second)

        return carry

    lax.fori_loop(0, UNITS + 3, step, 0)

    for p in range(2):
        for copy in (own_x, own_near, side_near, second_x, third_x):
            copy(p).wait_send()

    @pl.when(is_inner)
    def _():
        for p in range(2):
            for copy in (own_across, near_across, far_near, across_near):
                copy(p).wait_send()

    for u in range(UNITS):
        if u:
            weight(u).wait_send()
        core_copy(u).wait_send()
        y_copy(u).wait_send()
        hid_copy(u).wait_send()

    stage_e(third)
    over_copy().wait_recv()
    x_out[0] = (over[0].astype(F32) + over[2].astype(F32)).astype(BF16)
    x_copy(0).start()
    over_copy().wait_send()
    for d in range(1, NZ):
        z_copy(d).wait_send()
    x_copy(2).wait_send()
    x_copy(3).wait_send()

    total = acc[0]
    for d in range(1, NZ):
        z_copy(d).wait_recv()
        total = total + z_in[d].astype(F32)
    x_copy(0).wait_recv()
    out[...] = (total + x_in[0].astype(F32)).astype(BF16)
    x_copy(0).wait_send()


def dense(tokens, route_ids, gate_scores, up_weight, down_weight):
    rows, features = tokens.shape
    hidden = up_weight.shape[2]
    half = hidden // 2
    vmem = pl.BlockSpec(memory_space=pltpu.VMEM)
    hbm = pl.BlockSpec(memory_space=pltpu.HBM)
    dma = pltpu.SemaphoreType.DMA
    return pl.pallas_call(
        dense_kernel,
        out_shape=jax.ShapeDtypeStruct((rows, features), BF16),
        in_specs=[hbm, vmem, vmem, hbm, hbm],
        out_specs=vmem,
        scratch_shapes=[
            pltpu.VMEM((UNITS, rows, features), BF16),
            pltpu.VMEM((2, features, half), BF16),
            pltpu.VMEM((2, half, features), BF16),
            pltpu.VMEM((UNITS, UNITS, rows), F32),
            pltpu.VMEM((UNITS, rows, half), BF16),
            pltpu.VMEM((UNITS, rows, half), BF16),
            pltpu.VMEM((UNITS, rows, half), F32),
            pltpu.VMEM((UNITS, rows, half), BF16),
            pltpu.VMEM((UNITS, rows, half), BF16),
            pltpu.VMEM((UNITS, 2, rows, half), BF16),
            pltpu.VMEM((NZ, rows, features), F32),
            pltpu.VMEM((3, rows, features), BF16),
            pltpu.VMEM((NZ, rows, features), BF16),
            pltpu.VMEM((NZ, rows, features), BF16),
            pltpu.VMEM((NZ, rows, features), BF16),
            pltpu.VMEM((NZ, rows, features), BF16),
        ] + [dma((9, 2)), dma((UNITS, 2))] + [dma((UNITS,))] * 8 + [dma((NZ,))] * 4 + [dma((5,))],
        compiler_params=pltpu.CompilerParams(
            collective_id=0, has_side_effects=True, vmem_limit_bytes=63 * 2**20
        ),
        cost_estimate=pl.CostEstimate(
            flops=4 * UNITS * rows * features * hidden,
            bytes_accessed=4 * features * hidden + 4 * rows * features,
            transcendentals=UNITS * rows * half,
        ),
    )(tokens, route_ids.T, gate_scores.T, up_weight, down_weight)


def local(tokens, route_ids, gate_scores, up_weight, down_weight):
    experts = lax.axis_size("expert")
    every = route_ids.shape[1] == experts == UNITS and lax.axis_size("dp") == 4
    body = dense if every and tokens.shape[0] == 128 else routed
    return body(tokens, route_ids, gate_scores, up_weight, down_weight)


def solution(mesh):
    return jax.shard_map(
        local,
        mesh=mesh,
        in_specs=(
            P("expert", "dp"),
            P("expert", None),
            P("expert", None),
            P("expert", "dp", None),
            P("expert", None, "dp"),
        ),
        out_specs=P("expert", "dp"),
        check_vma=False,
    )
```

```python
import functools

import jax
import jax.numpy as jnp
from jax import lax
from jax.experimental import pallas as pl
from jax.experimental.pallas import tpu as pltpu
from jax.sharding import PartitionSpec as P

HOT = 2


ROUTE_SCALE = 2.5


def silu_hidden(before):
    summed = lax.psum(before.astype(jnp.bfloat16), "dp").astype(jnp.float32)
    result = jax.nn.silu(summed).astype(jnp.bfloat16)
    return result


def routed(tokens, route_ids, gate_scores, up_weight, down_weight):
    token_count, chosen_count = route_ids.shape
    features = tokens.shape[1]
    experts = lax.axis_size("expert")
    mean_rows = token_count * chosen_count // experts
    hot_most = min(2 * mean_rows - 1, token_count)
    cold_rows = (experts - HOT) * mean_rows - HOT * (hot_most - mean_rows)
    cold_most = -(-cold_rows // (experts - HOT))
    flat_ids = route_ids.reshape(-1)
    row_total = flat_ids.shape[0]
    expert_range = jnp.arange(experts, dtype=jnp.int32)
    onehot = (flat_ids[:, None] == expert_range[None, :]).astype(jnp.int32)
    running = jnp.cumsum(onehot, axis=0) - 1
    row_ranks = jnp.sum(onehot * running, axis=1)
    padded = jnp.concatenate([tokens, jnp.zeros((1, features), tokens.dtype)], axis=0)
    up_local = up_weight[0]
    down_local = down_weight[0]
    mix_weights = gate_scores * (ROUTE_SCALE / jnp.sum(gate_scores, axis=1, keepdims=True))
    slot_count = max(hot_most, cold_most)
    slot_of_row = flat_ids * slot_count + row_ranks
    slot_table = jnp.full((experts * slot_count,), row_total, jnp.int32)
    slot_table = slot_table.at[slot_of_row].set(jnp.arange(row_total, dtype=jnp.int32), mode="drop")
    sending = padded[slot_table // chosen_count].reshape(experts, slot_count, features)
    arrived = lax.all_to_all(sending, "expert", split_axis=0, concat_axis=0, tiled=True)
    item_count = arrived.shape[1]
    flat_rows = arrived.reshape(-1, features)
    before = jnp.dot(flat_rows, up_local, preferred_element_type=jnp.float32)
    hidden = silu_hidden(before)
    output = jnp.dot(hidden, down_local, preferred_element_type=jnp.float32)
    outcome = output.astype(jnp.bfloat16).reshape(experts, item_count, features)
    returned = lax.all_to_all(outcome, "expert", split_axis=0, concat_axis=0, tiled=True).reshape(
        -1, features
    )
    picked = returned[slot_of_row]
    picked = picked.reshape(token_count, chosen_count, features).astype(jnp.float32)
    mixed = jnp.sum(mix_weights[:, :, None] * picked, axis=1)
    return mixed.astype(jnp.bfloat16)


MESH = pl.DeviceIdType.MESH
F32 = jnp.float32
BF16 = jnp.bfloat16
NZ, NX = 4, 2
UNITS = NZ * NX


def mesh_xor(z, d):
    high = lax.rem(lax.div(z, 2) + lax.div(d, 2), 2)
    low = lax.rem(lax.rem(z, 2) + lax.rem(d, 2), 2)
    return high * 2 + low


def dense_kernel(
    tokens, route, gate, up, down, out,
    got, upv, downv, wt, core_out, core_in, kept, y_out, y_in, hid, hid_in, acc, res, over, x_out, x_in, z_out, z_in,
    tok_s, tok_r, w_s, w_r, core_s, core_r, y_s, y_r, hid_s, hid_r, x_s, x_r, z_s, z_r, load,
):
    expert = lax.axis_index("expert")
    part = lax.axis_index("dp")
    z, x = lax.div(expert, NX), lax.rem(expert, NX)
    y, core = lax.div(part, 2), lax.rem(part, 2)
    half = upv.shape[2]
    rows = tokens.shape[0]

    def at(d, other):
        xx = 1 - x if other else x
        return {"expert": mesh_xor(z, d) * NX + xx}

    x_peer = {"expert": z * NX + 1 - x}
    core_peer = {"dp": y * 2 + 1 - core}
    y_peer = {"dp": (1 - y) * 2 + core}

    def remote(src, dst, send, recv, device):
        return pltpu.make_async_remote_copy(
            src_ref=src, dst_ref=dst, send_sem=send, recv_sem=recv,
            device_id=device, device_id_type=MESH,
        )

    inner = lax.rem(mesh_xor(z, lax.div(z, 2)), 2)
    is_inner = inner == 1
    near, across = at(1, False), at(3, False)

    def token(k, src, slot, device):
        return remote(src, got.at[slot], tok_s.at[k], tok_r.at[slot], device)

    def token_in(u):
        return remote(tokens, got.at[u], tok_s.at[0], tok_r.at[u], x_peer)

    second, third = 2 + inner, 3 - inner
    own_x = token(0, tokens, 2, x_peer)
    own_near = token(1, tokens, 1, near)
    own_across = token(2, tokens, 3, across)
    near_across = token(3, got.at[1], 5, across)
    side_near = token(4, got.at[2], 6, near)
    across_near = token(5, got.at[3], 3, near)
    far_near = token(6, got.at[5], 5, near)
    second_x = token(7, got.at[3], 4, x_peer)
    third_x = token(8, got.at[5], 7, x_peer)

    def weight(k):
        return remote(wt.at[0], wt.at[k], w_s.at[k], w_r.at[k], at(k // 2, k % 2 == 1))

    def weight_in(u):
        return remote(wt.at[0], wt.at[u], w_s.at[u], w_r.at[u], x_peer)

    def core_copy(g):
        pair = pl.ds(2 * g, 2)
        return remote(core_out.at[pair], core_in.at[pair], core_s.at[g], core_r.at[g], core_peer)

    def y_copy(u):
        return remote(y_out.at[u], y_in.at[u], y_s.at[u], y_r.at[u], y_peer)

    def hid_copy(u):
        return remote(hid.at[u], hid_in.at[u], hid_s.at[u], hid_r.at[u], core_peer)

    def x_copy(d):
        return remote(x_out.at[d], x_in.at[d], x_s.at[d], x_r.at[d], x_peer)

    def over_copy():
        return remote(over.at[1], over.at[2], z_s.at[0], z_r.at[0], near)

    def z_copy(d):
        return remote(z_out.at[d], z_in.at[d], z_s.at[d], z_r.at[d], at(d, False))

    own = pl.ds(pl.multiple_of(core * half, half), half)
    theirs = pl.ds(pl.multiple_of((1 - core) * half, half), half)
    loads = [
        pltpu.make_async_copy(tokens, got.at[0], load.at[0]),
        pltpu.make_async_copy(up.at[0, :, theirs], upv.at[1], load.at[1]),
        pltpu.make_async_copy(up.at[0, :, own], upv.at[0], load.at[2]),
        pltpu.make_async_copy(down.at[0, own, :], downv.at[0], load.at[3]),
        pltpu.make_async_copy(down.at[0, theirs, :], downv.at[1], load.at[4]),
    ]
    for copy in loads:
        copy.start()

    barrier = pltpu.get_barrier_semaphore()
    peers = [at(k // 2, k % 2 == 1) for k in range(1, UNITS)] + [core_peer, y_peer]
    for peer in peers:
        pl.semaphore_signal(barrier, inc=1, device_id=peer, device_id_type=MESH)
    pl.semaphore_wait(barrier, len(peers))

    own_x.start()
    own_near.start()

    @pl.when(is_inner)
    def _():
        own_across.start()

    scores = gate[...]
    mix = scores * (ROUTE_SCALE / jnp.sum(scores, axis=0, keepdims=True))
    ids = route[...]
    named = lax.broadcasted_iota(jnp.int32, (UNITS, rows), 0)
    spread = jnp.zeros((UNITS, rows), F32)
    for k in range(UNITS):
        spread = spread + jnp.where(ids[k:k + 1, :] == named, mix[k:k + 1, :], 0.0)
    wt[0] = spread
    for k in range(1, UNITS):
        weight(k).start()
    for copy in loads:
        copy.wait()

    def arrivals(g):
        @pl.when(g == 0)
        def _():
            token_in(1).wait_recv()

            @pl.when(is_inner)
            def _():
                near_across.start()
                token_in(3).wait_recv()
                across_near.start()
                second_x.start()

        @pl.when(g == 1)
        def _():
            token_in(2).wait_recv()

            @pl.when(is_inner)
            def _():
                token_in(5).wait_recv()
                far_near.start()
                side_near.start()
                third_x.start()

            @pl.when(jnp.logical_not(is_inner))
            def _():
                side_near.start()
                token_in(3).wait_recv()
                second_x.start()

        @pl.when(g == 2)
        def _():
            @pl.when(jnp.logical_not(is_inner))
            def _():
                token_in(5).wait_recv()
                third_x.start()

            token_in(4).wait_recv()

        @pl.when(g == 3)
        def _():
            token_in(6).wait_recv()
            token_in(7).wait_recv()

    def stage_a(g):
        pair = pl.ds(2 * g, 2)
        block = got[pair].reshape(2 * rows, got.shape[2])
        theirs_sum = jnp.dot(block, upv[1], preferred_element_type=F32)
        core_out[pair] = theirs_sum.astype(BF16).reshape(2, rows, half)
        core_copy(g).start()
        kept[pair] = jnp.dot(block, upv[0], preferred_element_type=F32).reshape(2, rows, half)

    def stage_b(g):
        core_copy(g).wait_recv()
        for u in (2 * g, 2 * g + 1):
            total = kept[u] + core_in[u].astype(F32)
            kept[u] = total
            y_out[u] = total.astype(BF16)
            y_copy(u).start()

    def stage_c(g):
        for u in (2 * g, 2 * g + 1):
            y_copy(u).wait_recv()
            before = kept[u] + y_in[u].astype(F32)
            hid[u] = (before / (1.0 + jnp.exp(-before))).astype(BF16)
            hid_copy(u).start()

    places = [0, 2, 1, 2 * second, 2 * second + 1, 2 * third, 3, 2 * third + 1]

    def scale_of(u):
        k = places[7]
        for position in range(UNITS - 1):
            k = jnp.where(u == position, places[position], k)

        @pl.when(u >= 1)
        def _():
            weight_in(k).wait_recv()

        return jnp.broadcast_to(wt[k, pl.ds(expert, 1), :], (128, rows)).T

    def stage_d(g):
        pair = pl.ds(2 * g, 2)
        scale = jnp.concatenate([scale_of(2 * g), scale_of(2 * g + 1)], axis=0)
        hid_copy(2 * g).wait_recv()
        hid_copy(2 * g + 1).wait_recv()
        columns = res.shape[2]
        result = jnp.dot(hid[pair].reshape(2 * rows, half), downv[0], preferred_element_type=F32)
        result = result + jnp.dot(hid_in[pair].reshape(2 * rows, half), downv[1], preferred_element_type=F32)
        result = result * jnp.concatenate([scale] * (columns // 128), axis=1)
        res[...] = result.reshape(2, rows, columns)

        @pl.when(g == 0)
        def _():
            z_out[1] = res[1].astype(BF16)

            @pl.when(jnp.logical_not(is_inner))
            def _():
                z_copy(1).start()

            acc[0] = res[0]

        @pl.when(g == 1)
        def _():
            over[0] = res[0].astype(BF16)
            acc[second] = res[1]

        @pl.when(g == 2)
        def _():
            x_out[second] = res[0].astype(BF16)
            x_copy(second).start()
            acc[third] = res[1]

        @pl.when(g == 3)
        def _():
            x_out[third] = res[1].astype(BF16)
            x_copy(third).start()
            over[1] = res[0].astype(BF16)
            over_copy().start()

    def stage_e(d):
        x_copy(d).wait_recv()
        z_out[d] = (acc[d] + x_in[d].astype(F32)).astype(BF16)
        z_copy(d).start()

    pairs = UNITS // 2

    def step(t, carry):
        @pl.when(t < pairs)
        def _():
            arrivals(t)
            stage_a(t)
            stage_b(t)

        @pl.when((t == 3) & is_inner)
        def _():
            z_copy(1).start()

        @pl.when(t >= 1)
        def _():
            stage_c(t - 1)
            stage_d(t - 1)

        return carry

    lax.fori_loop(0, pairs + 1, step, 0)

    stage_e(second)
    stage_e(third)
    over_copy().wait_recv()
    x_out[0] = (over[0].astype(F32) + over[2].astype(F32)).astype(BF16)
    x_copy(0).start()

    for copy in (own_x, own_near, side_near, second_x, third_x):
        copy.wait_send()

    @pl.when(is_inner)
    def _():
        for copy in (own_across, near_across, far_near, across_near):
            copy.wait_send()

    for u in range(UNITS):
        if u:
            weight(u).wait_send()
        y_copy(u).wait_send()
        hid_copy(u).wait_send()
    for g in range(pairs):
        core_copy(g).wait_send()
    over_copy().wait_send()
    for d in range(1, NZ):
        z_copy(d).wait_send()
    x_copy(2).wait_send()
    x_copy(3).wait_send()

    total = acc[0]
    for d in range(1, NZ):
        z_copy(d).wait_recv()
        total = total + z_in[d].astype(F32)
    x_copy(0).wait_recv()
    out[...] = (total + x_in[0].astype(F32)).astype(BF16)
    x_copy(0).wait_send()


def dense(tokens, route_ids, gate_scores, up_weight, down_weight):
    rows, features = tokens.shape
    hidden = up_weight.shape[2]
    half = hidden // 2
    vmem = pl.BlockSpec(memory_space=pltpu.VMEM)
    hbm = pl.BlockSpec(memory_space=pltpu.HBM)
    dma = pltpu.SemaphoreType.DMA
    return pl.pallas_call(
        dense_kernel,
        out_shape=jax.ShapeDtypeStruct((rows, features), BF16),
        in_specs=[hbm, vmem, vmem, hbm, hbm],
        out_specs=vmem,
        scratch_shapes=[
            pltpu.VMEM((UNITS, rows, features), BF16),
            pltpu.VMEM((2, features, half), BF16),
            pltpu.VMEM((2, half, features), BF16),
            pltpu.VMEM((UNITS, UNITS, rows), F32),
            pltpu.VMEM((UNITS, rows, half), BF16),
            pltpu.VMEM((UNITS, rows, half), BF16),
            pltpu.VMEM((UNITS, rows, half), F32),
            pltpu.VMEM((UNITS, rows, half), BF16),
            pltpu.VMEM((UNITS, rows, half), BF16),
            pltpu.VMEM((UNITS, rows, half), BF16),
            pltpu.VMEM((UNITS, rows, half), BF16),
            pltpu.VMEM((NZ, rows, features), F32),
            pltpu.VMEM((2, rows, features), F32),
            pltpu.VMEM((3, rows, features), BF16),
            pltpu.VMEM((NZ, rows, features), BF16),
            pltpu.VMEM((NZ, rows, features), BF16),
            pltpu.VMEM((NZ, rows, features), BF16),
            pltpu.VMEM((NZ, rows, features), BF16),
        ] + [dma((9,))] + [dma((UNITS,))] * 9 + [dma((NZ,))] * 4 + [dma((5,))],
        compiler_params=pltpu.CompilerParams(
            collective_id=0, has_side_effects=True, vmem_limit_bytes=63 * 2**20
        ),
        cost_estimate=pl.CostEstimate(
            flops=4 * UNITS * rows * features * hidden,
            bytes_accessed=4 * features * hidden + 4 * rows * features,
            transcendentals=UNITS * rows * half,
        ),
    )(tokens, route_ids.T, gate_scores.T, up_weight, down_weight)


def local(tokens, route_ids, gate_scores, up_weight, down_weight):
    experts = lax.axis_size("expert")
    every = route_ids.shape[1] == experts == UNITS and lax.axis_size("dp") == 4
    body = dense if every and tokens.shape[0] == 128 else routed
    return body(tokens, route_ids, gate_scores, up_weight, down_weight)


def solution(mesh):
    return jax.shard_map(
        local,
        mesh=mesh,
        in_specs=(
            P("expert", "dp"),
            P("expert", None),
            P("expert", None),
            P("expert", "dp", None),
            P("expert", None, "dp"),
        ),
        out_specs=P("expert", "dp"),
        check_vma=False,
    )
```

```python
import functools

import jax
import jax.numpy as jnp
from jax import lax
from jax.experimental import pallas as pl
from jax.experimental.pallas import tpu as pltpu
from jax.sharding import PartitionSpec as P

HOT = 2


ROUTE_SCALE = 2.5


def silu_hidden(before):
    summed = lax.psum(before.astype(jnp.bfloat16), "dp").astype(jnp.float32)
    result = jax.nn.silu(summed).astype(jnp.bfloat16)
    return result


def routed(tokens, route_ids, gate_scores, up_weight, down_weight):
    token_count, chosen_count = route_ids.shape
    features = tokens.shape[1]
    experts = lax.axis_size("expert")
    mean_rows = token_count * chosen_count // experts
    hot_most = min(2 * mean_rows - 1, token_count)
    cold_rows = (experts - HOT) * mean_rows - HOT * (hot_most - mean_rows)
    cold_most = -(-cold_rows // (experts - HOT))
    flat_ids = route_ids.reshape(-1)
    row_total = flat_ids.shape[0]
    expert_range = jnp.arange(experts, dtype=jnp.int32)
    onehot = (flat_ids[:, None] == expert_range[None, :]).astype(jnp.int32)
    running = jnp.cumsum(onehot, axis=0) - 1
    row_ranks = jnp.sum(onehot * running, axis=1)
    padded = jnp.concatenate([tokens, jnp.zeros((1, features), tokens.dtype)], axis=0)
    up_local = up_weight[0]
    down_local = down_weight[0]
    mix_weights = gate_scores * (ROUTE_SCALE / jnp.sum(gate_scores, axis=1, keepdims=True))
    slot_count = max(hot_most, cold_most)
    slot_of_row = flat_ids * slot_count + row_ranks
    slot_table = jnp.full((experts * slot_count,), row_total, jnp.int32)
    slot_table = slot_table.at[slot_of_row].set(jnp.arange(row_total, dtype=jnp.int32), mode="drop")
    sending = padded[slot_table // chosen_count].reshape(experts, slot_count, features)
    arrived = lax.all_to_all(sending, "expert", split_axis=0, concat_axis=0, tiled=True)
    item_count = arrived.shape[1]
    flat_rows = arrived.reshape(-1, features)
    before = jnp.dot(flat_rows, up_local, preferred_element_type=jnp.float32)
    hidden = silu_hidden(before)
    output = jnp.dot(hidden, down_local, preferred_element_type=jnp.float32)
    outcome = output.astype(jnp.bfloat16).reshape(experts, item_count, features)
    returned = lax.all_to_all(outcome, "expert", split_axis=0, concat_axis=0, tiled=True).reshape(
        -1, features
    )
    picked = returned[slot_of_row]
    picked = picked.reshape(token_count, chosen_count, features).astype(jnp.float32)
    mixed = jnp.sum(mix_weights[:, :, None] * picked, axis=1)
    return mixed.astype(jnp.bfloat16)


MESH = pl.DeviceIdType.MESH
F32 = jnp.float32
BF16 = jnp.bfloat16
NZ, NX = 4, 2
UNITS = NZ * NX


def mesh_xor(z, d):
    high = lax.rem(lax.div(z, 2) + lax.div(d, 2), 2)
    low = lax.rem(lax.rem(z, 2) + lax.rem(d, 2), 2)
    return high * 2 + low


def dense_kernel(
    tokens, route, gate, up, down, out,
    got, upv, downv, wt, core_out, core_in, kept, y_out, y_in, hid, acc, x_out, x_in, z_out, z_in,
    tok_s, tok_r, w_s, w_r, core_s, core_r, y_s, y_r, hid_s, hid_r, x_s, x_r, z_s, z_r, load,
):
    expert = lax.axis_index("expert")
    part = lax.axis_index("dp")
    z, x = lax.div(expert, NX), lax.rem(expert, NX)
    y, core = lax.div(part, 2), lax.rem(part, 2)
    half = upv.shape[2]
    rows = tokens.shape[0]

    def at(d, other):
        xx = 1 - x if other else x
        return {"expert": mesh_xor(z, d) * NX + xx}

    x_peer = {"expert": z * NX + 1 - x}
    core_peer = {"dp": y * 2 + 1 - core}
    y_peer = {"dp": (1 - y) * 2 + core}

    def remote(src, dst, send, recv, device):
        return pltpu.make_async_remote_copy(
            src_ref=src, dst_ref=dst, send_sem=send, recv_sem=recv,
            device_id=device, device_id_type=MESH,
        )

    inner = lax.rem(mesh_xor(z, lax.div(z, 2)), 2)
    is_inner = inner == 1
    near, across = at(1, False), at(3, False)

    def token(k, src, slot, device):
        return remote(src, got.at[slot], tok_s.at[k], tok_r.at[slot], device)

    def token_in(u):
        return remote(tokens, got.at[u], tok_s.at[0], tok_r.at[u], x_peer)

    second, third = 2 + inner, 3 - inner
    own_x = token(0, tokens, 2, x_peer)
    own_near = token(1, tokens, 1, near)
    own_across = token(2, tokens, 3, across)
    near_across = token(3, got.at[1], 5, across)
    side_near = token(4, got.at[2], 6, near)
    across_near = token(5, got.at[3], 3, near)
    far_near = token(6, got.at[5], 5, near)
    second_x = token(7, got.at[3], 4, x_peer)
    third_x = token(8, got.at[5], 7, x_peer)

    def weight(k):
        return remote(wt.at[0], wt.at[k], w_s.at[k], w_r.at[k], at(k // 2, k % 2 == 1))

    def weight_in(u):
        return remote(wt.at[0], wt.at[u], w_s.at[u], w_r.at[u], x_peer)

    def core_copy(u):
        return remote(core_out.at[u], core_in.at[u], core_s.at[u], core_r.at[u], core_peer)

    def y_copy(u):
        return remote(y_out.at[u], y_in.at[u], y_s.at[u], y_r.at[u], y_peer)

    def hid_copy(u):
        return remote(hid.at[u, 0], hid.at[u, 1], hid_s.at[u], hid_r.at[u], core_peer)

    def x_copy(d):
        return remote(x_out.at[d], x_in.at[d], x_s.at[d], x_r.at[d], x_peer)

    def z_copy(d):
        return remote(z_out.at[d], z_in.at[d], z_s.at[d], z_r.at[d], at(d, False))

    own = pl.ds(pl.multiple_of(core * half, half), half)
    theirs = pl.ds(pl.multiple_of((1 - core) * half, half), half)
    loads = [
        pltpu.make_async_copy(tokens, got.at[0], load.at[0]),
        pltpu.make_async_copy(up.at[0, :, theirs], upv.at[1], load.at[1]),
        pltpu.make_async_copy(up.at[0, :, own], upv.at[0], load.at[2]),
        pltpu.make_async_copy(down.at[0, own, :], downv.at[0], load.at[3]),
        pltpu.make_async_copy(down.at[0, theirs, :], downv.at[1], load.at[4]),
    ]
    for copy in loads:
        copy.start()

    barrier = pltpu.get_barrier_semaphore()
    peers = [at(k // 2, k % 2 == 1) for k in range(1, UNITS)] + [core_peer, y_peer]
    for peer in peers:
        pl.semaphore_signal(barrier, inc=1, device_id=peer, device_id_type=MESH)
    pl.semaphore_wait(barrier, len(peers))

    own_x.start()
    own_near.start()

    @pl.when(is_inner)
    def _():
        own_across.start()

    scores = gate[...]
    mix = scores * (ROUTE_SCALE / jnp.sum(scores, axis=0, keepdims=True))
    ids = route[...]
    named = lax.broadcasted_iota(jnp.int32, (UNITS, rows), 0)
    spread = jnp.zeros((UNITS, rows), F32)
    for k in range(UNITS):
        spread = spread + jnp.where(ids[k:k + 1, :] == named, mix[k:k + 1, :], 0.0)
    wt[0] = spread
    for k in range(1, UNITS):
        weight(k).start()
    for copy in loads:
        copy.wait()

    def first_arrivals():
        token_in(1).wait_recv()

        @pl.when(is_inner)
        def _():
            near_across.start()
            token_in(3).wait_recv()
            across_near.start()
            second_x.start()

        token_in(2).wait_recv()

        @pl.when(jnp.logical_not(is_inner))
        def _():
            side_near.start()

    def second_arrivals():
        @pl.when(is_inner)
        def _():
            token_in(5).wait_recv()
            far_near.start()
            side_near.start()
            third_x.start()

        @pl.when(jnp.logical_not(is_inner))
        def _():
            token_in(3).wait_recv()
            second_x.start()

    def third_arrivals():
        @pl.when(jnp.logical_not(is_inner))
        def _():
            token_in(5).wait_recv()
            third_x.start()

        token_in(4).wait_recv()

    def stage_a(u):
        @pl.when(u >= 6)
        def _():
            token_in(u).wait_recv()

        block = got[u]
        core_out[u] = jnp.dot(block, upv[1], preferred_element_type=F32).astype(BF16)
        core_copy(u).start()
        kept[u] = jnp.dot(block, upv[0], preferred_element_type=F32)

    def stage_b(u):
        core_copy(u).wait_recv()
        total = kept[u] + core_in[u].astype(F32)
        kept[u] = total
        y_out[u] = total.astype(BF16)
        y_copy(u).start()

    def stage_c(u):
        y_copy(u).wait_recv()
        before = kept[u] + y_in[u].astype(F32)
        hid[u, 0] = (before / (1.0 + jnp.exp(-before))).astype(BF16)
        hid_copy(u).start()

    def stage_d(u):
        other = (u == 2) | (u == 4) | (u >= 6)
        d = jnp.where((u == 1) | (u == 6), 1, jnp.where((u == 3) | (u == 4), second, third))
        d = jnp.where((u == 0) | (u == 2), 0, d)
        k = 2 * d + other.astype(jnp.int32)

        @pl.when(u >= 1)
        def _():
            weight_in(k).wait_recv()

        scale = jnp.broadcast_to(wt[k, pl.ds(expert, 1), :], (128, rows)).T
        hid_copy(u).wait_recv()
        result = jnp.dot(hid[u, 0], downv[0], preferred_element_type=F32)
        result = result + jnp.dot(hid[u, 1], downv[1], preferred_element_type=F32)
        result = result * jnp.concatenate([scale] * (result.shape[1] // 128), axis=1)

        @pl.when(jnp.logical_not(other))
        def _():
            acc[d] = result

        @pl.when(other)
        def _():
            x_out[d] = result.astype(BF16)
            x_copy(d).start()

    def stage_e(d):
        x_copy(d).wait_recv()
        z_out[d] = (acc[d] + x_in[d].astype(F32)).astype(BF16)
        z_copy(d).start()

    def step(t, carry):
        @pl.when(t == 3)
        def _():
            second_arrivals()

        @pl.when(t == 4)
        def _():
            third_arrivals()

        @pl.when(t < UNITS)
        def _():
            stage_a(t)

        @pl.when((t >= 2) & (t < UNITS + 1))
        def _():
            stage_b(t - 1)

        @pl.when((t >= 2) & (t < UNITS + 2))
        def _():
            stage_c(t - 2)

        @pl.when((t >= 3) & (t < UNITS + 3))
        def _():
            stage_d(t - 3)

        @pl.when(t == 8)
        def _():
            stage_e(second)

        return carry

    stage_a(0)
    stage_b(0)
    first_arrivals()
    lax.fori_loop(1, UNITS + 3, step, 0)

    stage_e(1)
    stage_e(third)

    for copy in (own_x, own_near, side_near, second_x, third_x):
        copy.wait_send()

    @pl.when(is_inner)
    def _():
        for copy in (own_across, near_across, far_near, across_near):
            copy.wait_send()

    for u in range(UNITS):
        if u:
            weight(u).wait_send()
        core_copy(u).wait_send()
        y_copy(u).wait_send()
        hid_copy(u).wait_send()
    for d in range(NZ):
        x_copy(d).wait_send()

    x_copy(0).wait_recv()
    total = acc[0] + x_in[0].astype(F32)
    for d in (1, 2, 3):
        z_copy(d).wait_send()
    for d in (1, 2, 3):
        z_copy(d).wait_recv()
        total = total + z_in[d].astype(F32)
    out[...] = total.astype(BF16)


def dense(tokens, route_ids, gate_scores, up_weight, down_weight):
    rows, features = tokens.shape
    hidden = up_weight.shape[2]
    half = hidden // 2
    vmem = pl.BlockSpec(memory_space=pltpu.VMEM)
    hbm = pl.BlockSpec(memory_space=pltpu.HBM)
    dma = pltpu.SemaphoreType.DMA
    return pl.pallas_call(
        dense_kernel,
        out_shape=jax.ShapeDtypeStruct((rows, features), BF16),
        in_specs=[hbm, vmem, vmem, hbm, hbm],
        out_specs=vmem,
        scratch_shapes=[
            pltpu.VMEM((UNITS, rows, features), BF16),
            pltpu.VMEM((2, features, half), BF16),
            pltpu.VMEM((2, half, features), BF16),
            pltpu.VMEM((UNITS, UNITS, rows), F32),
            pltpu.VMEM((UNITS, rows, half), BF16),
            pltpu.VMEM((UNITS, rows, half), BF16),
            pltpu.VMEM((UNITS, rows, half), F32),
            pltpu.VMEM((UNITS, rows, half), BF16),
            pltpu.VMEM((UNITS, rows, half), BF16),
            pltpu.VMEM((UNITS, 2, rows, half), BF16),
            pltpu.VMEM((NZ, rows, features), F32),
            pltpu.VMEM((NZ, rows, features), BF16),
            pltpu.VMEM((NZ, rows, features), BF16),
            pltpu.VMEM((NZ, rows, features), BF16),
            pltpu.VMEM((NZ, rows, features), BF16),
        ] + [dma((9,))] + [dma((UNITS,))] * 9 + [dma((NZ,))] * 4 + [dma((5,))],
        compiler_params=pltpu.CompilerParams(
            collective_id=0, has_side_effects=True, vmem_limit_bytes=63 * 2**20
        ),
        cost_estimate=pl.CostEstimate(
            flops=4 * UNITS * rows * features * hidden,
            bytes_accessed=4 * features * hidden + 4 * rows * features,
            transcendentals=UNITS * rows * half,
        ),
    )(tokens, route_ids.T, gate_scores.T, up_weight, down_weight)


def local(tokens, route_ids, gate_scores, up_weight, down_weight):
    experts = lax.axis_size("expert")
    every = route_ids.shape[1] == experts == UNITS and lax.axis_size("dp") == 4
    body = dense if every and tokens.shape[0] == 128 else routed
    return body(tokens, route_ids, gate_scores, up_weight, down_weight)


def solution(mesh):
    return jax.shard_map(
        local,
        mesh=mesh,
        in_specs=(
            P("expert", "dp"),
            P("expert", None),
            P("expert", None),
            P("expert", "dp", None),
            P("expert", None, "dp"),
        ),
        out_specs=P("expert", "dp"),
        check_vma=False,
    )
```

```python
import functools

import jax
import jax.numpy as jnp
from jax import lax
from jax.experimental import pallas as pl
from jax.experimental.pallas import tpu as pltpu
from jax.sharding import PartitionSpec as P

HOT = 2


ROUTE_SCALE = 2.5


def silu_hidden(before):
    summed = lax.psum(before.astype(jnp.bfloat16), "dp").astype(jnp.float32)
    result = jax.nn.silu(summed).astype(jnp.bfloat16)
    return result


def routed(tokens, route_ids, gate_scores, up_weight, down_weight):
    token_count, chosen_count = route_ids.shape
    features = tokens.shape[1]
    experts = lax.axis_size("expert")
    mean_rows = token_count * chosen_count // experts
    hot_most = min(2 * mean_rows - 1, token_count)
    cold_rows = (experts - HOT) * mean_rows - HOT * (hot_most - mean_rows)
    cold_most = -(-cold_rows // (experts - HOT))
    flat_ids = route_ids.reshape(-1)
    row_total = flat_ids.shape[0]
    expert_range = jnp.arange(experts, dtype=jnp.int32)
    onehot = (flat_ids[:, None] == expert_range[None, :]).astype(jnp.int32)
    running = jnp.cumsum(onehot, axis=0) - 1
    row_ranks = jnp.sum(onehot * running, axis=1)
    padded = jnp.concatenate([tokens, jnp.zeros((1, features), tokens.dtype)], axis=0)
    up_local = up_weight[0]
    down_local = down_weight[0]
    mix_weights = gate_scores * (ROUTE_SCALE / jnp.sum(gate_scores, axis=1, keepdims=True))
    slot_count = max(hot_most, cold_most)
    slot_of_row = flat_ids * slot_count + row_ranks
    slot_table = jnp.full((experts * slot_count,), row_total, jnp.int32)
    slot_table = slot_table.at[slot_of_row].set(jnp.arange(row_total, dtype=jnp.int32), mode="drop")
    sending = padded[slot_table // chosen_count].reshape(experts, slot_count, features)
    arrived = lax.all_to_all(sending, "expert", split_axis=0, concat_axis=0, tiled=True)
    item_count = arrived.shape[1]
    flat_rows = arrived.reshape(-1, features)
    before = jnp.dot(flat_rows, up_local, preferred_element_type=jnp.float32)
    hidden = silu_hidden(before)
    output = jnp.dot(hidden, down_local, preferred_element_type=jnp.float32)
    outcome = output.astype(jnp.bfloat16).reshape(experts, item_count, features)
    returned = lax.all_to_all(outcome, "expert", split_axis=0, concat_axis=0, tiled=True).reshape(
        -1, features
    )
    picked = returned[slot_of_row]
    picked = picked.reshape(token_count, chosen_count, features).astype(jnp.float32)
    mixed = jnp.sum(mix_weights[:, :, None] * picked, axis=1)
    return mixed.astype(jnp.bfloat16)


MESH = pl.DeviceIdType.MESH
F32 = jnp.float32
BF16 = jnp.bfloat16
NZ, NX = 4, 2
UNITS = NZ * NX


def mesh_xor(z, d):
    high = lax.rem(lax.div(z, 2) + lax.div(d, 2), 2)
    low = lax.rem(lax.rem(z, 2) + lax.rem(d, 2), 2)
    return high * 2 + low


def dense_kernel(
    tokens, route, gate, up, down, out,
    got, upv, downv, wt, core_out, core_in, kept, y_out, y_in, hid, acc, over, x_out, x_in, z_out, z_in,
    tok_s, tok_r, w_s, w_r, core_s, core_r, y_s, y_r, hid_s, hid_r, x_s, x_r, z_s, z_r, load,
):
    expert = lax.axis_index("expert")
    part = lax.axis_index("dp")
    z, x = lax.div(expert, NX), lax.rem(expert, NX)
    y, core = lax.div(part, 2), lax.rem(part, 2)
    half = upv.shape[2]
    rows = tokens.shape[0]

    def at(d, other):
        xx = 1 - x if other else x
        return {"expert": mesh_xor(z, d) * NX + xx}

    x_peer = {"expert": z * NX + 1 - x}
    core_peer = {"dp": y * 2 + 1 - core}
    y_peer = {"dp": (1 - y) * 2 + core}

    def remote(src, dst, send, recv, device):
        return pltpu.make_async_remote_copy(
            src_ref=src, dst_ref=dst, send_sem=send, recv_sem=recv,
            device_id=device, device_id_type=MESH,
        )

    inner = lax.rem(mesh_xor(z, lax.div(z, 2)), 2)
    is_inner = inner == 1
    near, across = at(1, False), at(3, False)

    def token(k, src, slot, device):
        def piece(p):
            return remote(
                src.at[lines(p)], got.at[slot, lines(p)], tok_s.at[k, p], tok_r.at[slot, p], device)
        return piece

    def token_in(u, p):
        return remote(tokens.at[lines(p)], got.at[u, lines(p)], tok_s.at[0, p], tok_r.at[u, p], x_peer)

    second, third = 2 + inner, 3 - inner
    own_x = token(0, tokens, 2, x_peer)
    own_near = token(1, tokens, 1, near)
    own_across = token(2, tokens, 3, across)
    near_across = token(3, got.at[1], 5, across)
    side_near = token(4, got.at[2], 6, near)
    across_near = token(5, got.at[3], 3, near)
    far_near = token(6, got.at[5], 5, near)
    second_x = token(7, got.at[3], 4, x_peer)
    third_x = token(8, got.at[5], 7, x_peer)

    def weight(k):
        return remote(wt.at[0], wt.at[k], w_s.at[k], w_r.at[k], at(k // 2, k % 2 == 1))

    def weight_in(u):
        return remote(wt.at[0], wt.at[u], w_s.at[u], w_r.at[u], x_peer)

    def core_copy(u):
        return remote(core_out.at[u], core_in.at[u], core_s.at[u], core_r.at[u], core_peer)

    def y_copy(u):
        return remote(y_out.at[u], y_in.at[u], y_s.at[u], y_r.at[u], y_peer)

    def hid_copy(u):
        return remote(hid.at[u, 0], hid.at[u, 1], hid_s.at[u], hid_r.at[u], core_peer)

    part_rows = rows // 2

    def lines(p):
        return pl.ds(p * part_rows, part_rows)

    def x_copy(d, p):
        return remote(x_out.at[d, lines(p)], x_in.at[d, lines(p)], x_s.at[d, p], x_r.at[d, p], x_peer)

    def over_copy(p):
        return remote(over.at[1, lines(p)], over.at[2, lines(p)], z_s.at[0, p], z_r.at[0, p], near)

    def z_copy(d, p):
        return remote(z_out.at[d, lines(p)], z_in.at[d, lines(p)], z_s.at[d, p], z_r.at[d, p], at(d, False))

    own = pl.ds(pl.multiple_of(core * half, half), half)
    theirs = pl.ds(pl.multiple_of((1 - core) * half, half), half)
    loads = [
        pltpu.make_async_copy(tokens, got.at[0], load.at[0]),
        pltpu.make_async_copy(up.at[0, :, theirs], upv.at[1], load.at[1]),
        pltpu.make_async_copy(up.at[0, :, own], upv.at[0], load.at[2]),
        pltpu.make_async_copy(down.at[0, own, :], downv.at[0], load.at[3]),
        pltpu.make_async_copy(down.at[0, theirs, :], downv.at[1], load.at[4]),
    ]
    for copy in loads:
        copy.start()

    barrier = pltpu.get_barrier_semaphore()
    peers = [at(k // 2, k % 2 == 1) for k in range(1, UNITS)] + [core_peer, y_peer]
    for peer in peers:
        pl.semaphore_signal(barrier, inc=1, device_id=peer, device_id_type=MESH)
    pl.semaphore_wait(barrier, len(peers))

    own_x(0).start()
    own_near(0).start()

    @pl.when(is_inner)
    def _():
        own_across(0).start()

    own_x(1).start()
    own_near(1).start()

    @pl.when(is_inner)
    def _():
        own_across(1).start()

    scores = gate[...]
    mix = scores * (ROUTE_SCALE / jnp.sum(scores, axis=0, keepdims=True))
    ids = route[...]
    named = lax.broadcasted_iota(jnp.int32, (UNITS, rows), 0)
    spread = jnp.zeros((UNITS, rows), F32)
    for k in range(UNITS):
        spread = spread + jnp.where(ids[k:k + 1, :] == named, mix[k:k + 1, :], 0.0)
    wt[0] = spread
    for k in range(1, UNITS):
        weight(k).start()
    for copy in loads:
        copy.wait()

    def first_arrivals():
        for p in range(2):
            token_in(1, p).wait_recv()

            @pl.when(is_inner)
            def _():
                near_across(p).start()
                token_in(3, p).wait_recv()
                across_near(p).start()
                second_x(p).start()

            token_in(2, p).wait_recv()

            @pl.when(jnp.logical_not(is_inner))
            def _():
                side_near(p).start()

    def second_arrivals():
        for p in range(2):
            @pl.when(is_inner)
            def _():
                token_in(5, p).wait_recv()
                far_near(p).start()
                third_x(p).start()

            @pl.when(jnp.logical_not(is_inner))
            def _():
                token_in(3, p).wait_recv()
                second_x(p).start()

        @pl.when(is_inner)
        def _():
            side_near(0).start()
            side_near(1).start()

    def third_arrivals():
        for p in range(2):
            @pl.when(jnp.logical_not(is_inner))
            def _():
                token_in(5, p).wait_recv()
                third_x(p).start()

        token_in(4, 0).wait_recv()
        token_in(4, 1).wait_recv()

    def stage_a(u):
        @pl.when(u >= 6)
        def _():
            token_in(u, 0).wait_recv()
            token_in(u, 1).wait_recv()

        block = got[u]
        core_out[u] = jnp.dot(block, upv[1], preferred_element_type=F32).astype(BF16)
        core_copy(u).start()
        kept[u] = jnp.dot(block, upv[0], preferred_element_type=F32)

    def stage_b(u):
        core_copy(u).wait_recv()
        total = kept[u] + core_in[u].astype(F32)
        kept[u] = total
        y_out[u] = total.astype(BF16)
        y_copy(u).start()

    def stage_c(u):
        y_copy(u).wait_recv()
        before = kept[u] + y_in[u].astype(F32)
        hid[u, 0] = (before / (1.0 + jnp.exp(-before))).astype(BF16)
        hid_copy(u).start()

    def stage_d(u):
        other = (u == 2) | (u == 4) | (u >= 6)
        d = jnp.where((u == 1) | (u == 6), 1, jnp.where((u == 3) | (u == 4), second, third))
        d = jnp.where((u == 0) | (u == 2), 0, d)
        k = 2 * d + other.astype(jnp.int32)

        @pl.when(u >= 1)
        def _():
            weight_in(k).wait_recv()

        scale = jnp.broadcast_to(wt[k, pl.ds(expert, 1), :], (128, rows)).T
        hid_copy(u).wait_recv()
        result = jnp.dot(hid[u, 0], downv[0], preferred_element_type=F32)
        result = result + jnp.dot(hid[u, 1], downv[1], preferred_element_type=F32)
        result = result * jnp.concatenate([scale] * (result.shape[1] // 128), axis=1)

        @pl.when((u == 0) | (u == 3) | (u == 5))
        def _():
            acc[d] = result

        @pl.when(u == 1)
        def _():
            z_out[1] = result.astype(BF16)
            z_copy(1, 0).start()
            z_copy(1, 1).start()

        @pl.when(u == 2)
        def _():
            over[0] = result.astype(BF16)

        @pl.when(u == 6)
        def _():
            over[1] = result.astype(BF16)
            over_copy(0).start()
            over_copy(1).start()

        @pl.when((u == 4) | (u == 7))
        def _():
            x_out[d] = result.astype(BF16)
            x_copy(d, 0).start()
            x_copy(d, 1).start()

    def stage_e(d, p):
        x_copy(d, p).wait_recv()
        z_out[d, lines(p)] = (acc[d, lines(p)] + x_in[d, lines(p)].astype(F32)).astype(BF16)
        z_copy(d, p).start()

    def step(t, carry):
        @pl.when(t == 3)
        def _():
            second_arrivals()

        @pl.when(t == 4)
        def _():
            third_arrivals()

        @pl.when(t < UNITS)
        def _():
            stage_a(t)

        @pl.when((t >= 2) & (t < UNITS + 1))
        def _():
            stage_b(t - 1)

        @pl.when((t >= 2) & (t < UNITS + 2))
        def _():
            stage_c(t - 2)

        @pl.when((t >= 3) & (t < UNITS + 3))
        def _():
            stage_d(t - 3)

        @pl.when(t == 8)
        def _():
            stage_e(second, 0)
            stage_e(second, 1)

        return carry

    stage_a(0)
    stage_b(0)
    first_arrivals()
    lax.fori_loop(1, UNITS + 3, step, 0)

    for p in range(2):
        for copy in (own_x, own_near, side_near, second_x, third_x):
            copy(p).wait_send()

    @pl.when(is_inner)
    def _():
        for p in range(2):
            for copy in (own_across, near_across, far_near, across_near):
                copy(p).wait_send()

    for u in range(UNITS):
        if u:
            weight(u).wait_send()
        core_copy(u).wait_send()
        y_copy(u).wait_send()
        hid_copy(u).wait_send()

    for p in range(2):
        stage_e(third, p)
        over_copy(p).wait_recv()
        x_out[0, lines(p)] = (over[0, lines(p)].astype(F32) + over[2, lines(p)].astype(F32)).astype(BF16)
        x_copy(0, p).start()

    for p in range(2):
        over_copy(p).wait_send()
        x_copy(2, p).wait_send()
        x_copy(3, p).wait_send()
        for d in range(1, NZ):
            z_copy(d, p).wait_send()

    for p in range(2):
        total = acc[0, lines(p)]
        for d in range(1, NZ):
            z_copy(d, p).wait_recv()
            total = total + z_in[d, lines(p)].astype(F32)
        x_copy(0, p).wait_recv()
        out[lines(p)] = (total + x_in[0, lines(p)].astype(F32)).astype(BF16)
    for p in range(2):
        x_copy(0, p).wait_send()


def dense(tokens, route_ids, gate_scores, up_weight, down_weight):
    rows, features = tokens.shape
    hidden = up_weight.shape[2]
    half = hidden // 2
    vmem = pl.BlockSpec(memory_space=pltpu.VMEM)
    hbm = pl.BlockSpec(memory_space=pltpu.HBM)
    dma = pltpu.SemaphoreType.DMA
    return pl.pallas_call(
        dense_kernel,
        out_shape=jax.ShapeDtypeStruct((rows, features), BF16),
        in_specs=[hbm, vmem, vmem, hbm, hbm],
        out_specs=vmem,
        scratch_shapes=[
            pltpu.VMEM((UNITS, rows, features), BF16),
            pltpu.VMEM((2, features, half), BF16),
            pltpu.VMEM((2, half, features), BF16),
            pltpu.VMEM((UNITS, UNITS, rows), F32),
            pltpu.VMEM((UNITS, rows, half), BF16),
            pltpu.VMEM((UNITS, rows, half), BF16),
            pltpu.VMEM((UNITS, rows, half), F32),
            pltpu.VMEM((UNITS, rows, half), BF16),
            pltpu.VMEM((UNITS, rows, half), BF16),
            pltpu.VMEM((UNITS, 2, rows, half), BF16),
            pltpu.VMEM((NZ, rows, features), F32),
            pltpu.VMEM((3, rows, features), BF16),
            pltpu.VMEM((NZ, rows, features), BF16),
            pltpu.VMEM((NZ, rows, features), BF16),
            pltpu.VMEM((NZ, rows, features), BF16),
            pltpu.VMEM((NZ, rows, features), BF16),
        ] + [dma((9, 2)), dma((UNITS, 2))] + [dma((UNITS,))] * 8 + [dma((NZ, 2))] * 4 + [dma((5,))],
        compiler_params=pltpu.CompilerParams(
            collective_id=0, has_side_effects=True, vmem_limit_bytes=63 * 2**20
        ),
        cost_estimate=pl.CostEstimate(
            flops=4 * UNITS * rows * features * hidden,
            bytes_accessed=4 * features * hidden + 4 * rows * features,
            transcendentals=UNITS * rows * half,
        ),
    )(tokens, route_ids.T, gate_scores.T, up_weight, down_weight)


def local(tokens, route_ids, gate_scores, up_weight, down_weight):
    experts = lax.axis_size("expert")
    every = route_ids.shape[1] == experts == UNITS and lax.axis_size("dp") == 4
    body = dense if every and tokens.shape[0] == 128 else routed
    return body(tokens, route_ids, gate_scores, up_weight, down_weight)


def solution(mesh):
    return jax.shard_map(
        local,
        mesh=mesh,
        in_specs=(
            P("expert", "dp"),
            P("expert", None),
            P("expert", None),
            P("expert", "dp", None),
            P("expert", None, "dp"),
        ),
        out_specs=P("expert", "dp"),
        check_vma=False,
    )
```

```python
import functools

import jax
import jax.numpy as jnp
from jax import lax
from jax.experimental import pallas as pl
from jax.experimental.pallas import tpu as pltpu
from jax.sharding import PartitionSpec as P

HOT = 2


ROUTE_SCALE = 2.5


def silu_hidden(before):
    summed = lax.psum(before.astype(jnp.bfloat16), "dp").astype(jnp.float32)
    result = jax.nn.silu(summed).astype(jnp.bfloat16)
    return result


def routed(tokens, route_ids, gate_scores, up_weight, down_weight):
    token_count, chosen_count = route_ids.shape
    features = tokens.shape[1]
    experts = lax.axis_size("expert")
    mean_rows = token_count * chosen_count // experts
    hot_most = min(2 * mean_rows - 1, token_count)
    cold_rows = (experts - HOT) * mean_rows - HOT * (hot_most - mean_rows)
    cold_most = -(-cold_rows // (experts - HOT))
    flat_ids = route_ids.reshape(-1)
    row_total = flat_ids.shape[0]
    expert_range = jnp.arange(experts, dtype=jnp.int32)
    onehot = (flat_ids[:, None] == expert_range[None, :]).astype(jnp.int32)
    running = jnp.cumsum(onehot, axis=0) - 1
    row_ranks = jnp.sum(onehot * running, axis=1)
    padded = jnp.concatenate([tokens, jnp.zeros((1, features), tokens.dtype)], axis=0)
    up_local = up_weight[0]
    down_local = down_weight[0]
    mix_weights = gate_scores * (ROUTE_SCALE / jnp.sum(gate_scores, axis=1, keepdims=True))
    slot_count = max(hot_most, cold_most)
    slot_of_row = flat_ids * slot_count + row_ranks
    slot_table = jnp.full((experts * slot_count,), row_total, jnp.int32)
    slot_table = slot_table.at[slot_of_row].set(jnp.arange(row_total, dtype=jnp.int32), mode="drop")
    sending = padded[slot_table // chosen_count].reshape(experts, slot_count, features)
    arrived = lax.all_to_all(sending, "expert", split_axis=0, concat_axis=0, tiled=True)
    item_count = arrived.shape[1]
    flat_rows = arrived.reshape(-1, features)
    before = jnp.dot(flat_rows, up_local, preferred_element_type=jnp.float32)
    hidden = silu_hidden(before)
    output = jnp.dot(hidden, down_local, preferred_element_type=jnp.float32)
    outcome = output.astype(jnp.bfloat16).reshape(experts, item_count, features)
    returned = lax.all_to_all(outcome, "expert", split_axis=0, concat_axis=0, tiled=True).reshape(
        -1, features
    )
    picked = returned[slot_of_row]
    picked = picked.reshape(token_count, chosen_count, features).astype(jnp.float32)
    mixed = jnp.sum(mix_weights[:, :, None] * picked, axis=1)
    return mixed.astype(jnp.bfloat16)


MESH = pl.DeviceIdType.MESH
F32 = jnp.float32
BF16 = jnp.bfloat16
NZ, NX = 4, 2
UNITS = NZ * NX


def mesh_xor(z, d):
    high = lax.rem(lax.div(z, 2) + lax.div(d, 2), 2)
    low = lax.rem(lax.rem(z, 2) + lax.rem(d, 2), 2)
    return high * 2 + low


def dense_kernel(
    tokens, route, gate, up, down, out,
    got, upv, downv, wt, core_out, core_in, kept, y_out, y_in, hid, acc, over, x_out, x_in, z_out, z_in,
    tok_s, tok_r, w_s, w_r, core_s, core_r, y_s, y_r, hid_s, hid_r, x_s, x_r, z_s, z_r, load,
):
    expert = lax.axis_index("expert")
    part = lax.axis_index("dp")
    z, x = lax.div(expert, NX), lax.rem(expert, NX)
    y, core = lax.div(part, 2), lax.rem(part, 2)
    half = upv.shape[2]
    rows = tokens.shape[0]

    def at(d, other):
        xx = 1 - x if other else x
        return {"expert": mesh_xor(z, d) * NX + xx}

    x_peer = {"expert": z * NX + 1 - x}
    core_peer = {"dp": y * 2 + 1 - core}
    y_peer = {"dp": (1 - y) * 2 + core}

    def remote(src, dst, send, recv, device):
        return pltpu.make_async_remote_copy(
            src_ref=src, dst_ref=dst, send_sem=send, recv_sem=recv,
            device_id=device, device_id_type=MESH,
        )

    inner = lax.rem(mesh_xor(z, lax.div(z, 2)), 2)
    is_inner = inner == 1
    near, across = at(1, False), at(3, False)

    def token(k, src, slot, device):
        def piece(p):
            return remote(
                src.at[lines(p)], got.at[slot, lines(p)], tok_s.at[k, p], tok_r.at[slot, p], device)
        return piece

    def token_in(u, p):
        return remote(tokens.at[lines(p)], got.at[u, lines(p)], tok_s.at[0, p], tok_r.at[u, p], x_peer)

    second, third = 2 + inner, 3 - inner
    own_x = token(0, tokens, 2, x_peer)
    own_near = token(1, tokens, 1, near)
    own_across = token(2, tokens, 3, across)
    near_across = token(3, got.at[1], 5, across)
    side_near = token(4, got.at[2], 6, near)
    across_near = token(5, got.at[3], 3, near)
    far_near = token(6, got.at[5], 5, near)
    second_x = token(7, got.at[3], 4, x_peer)
    third_x = token(8, got.at[5], 7, x_peer)
    near_x = token(9, got.at[1], 6, x_peer)

    def weight(k):
        return remote(wt.at[0], wt.at[k], w_s.at[k], w_r.at[k], at(k // 2, k % 2 == 1))

    def weight_in(u):
        return remote(wt.at[0], wt.at[u], w_s.at[u], w_r.at[u], x_peer)

    def core_copy(u):
        return remote(core_out.at[u], core_in.at[u], core_s.at[u], core_r.at[u], core_peer)

    def y_copy(u):
        return remote(y_out.at[u], y_in.at[u], y_s.at[u], y_r.at[u], y_peer)

    def hid_copy(u):
        return remote(hid.at[u, 0], hid.at[u, 1], hid_s.at[u], hid_r.at[u], core_peer)

    part_rows = rows // 2

    def lines(p):
        return pl.ds(p * part_rows, part_rows)

    def x_copy(d, p):
        return remote(x_out.at[d, lines(p)], x_in.at[d, lines(p)], x_s.at[d, p], x_r.at[d, p], x_peer)

    def over_copy(p):
        return remote(over.at[1, lines(p)], over.at[2, lines(p)], z_s.at[0, p], z_r.at[0, p], near)

    def z_copy(d, p):
        return remote(z_out.at[d, lines(p)], z_in.at[d, lines(p)], z_s.at[d, p], z_r.at[d, p], at(d, False))

    own = pl.ds(pl.multiple_of(core * half, half), half)
    theirs = pl.ds(pl.multiple_of((1 - core) * half, half), half)
    loads = [
        pltpu.make_async_copy(tokens, got.at[0], load.at[0]),
        pltpu.make_async_copy(up.at[0, :, theirs], upv.at[1], load.at[1]),
        pltpu.make_async_copy(up.at[0, :, own], upv.at[0], load.at[2]),
        pltpu.make_async_copy(down.at[0, own, :], downv.at[0], load.at[3]),
        pltpu.make_async_copy(down.at[0, theirs, :], downv.at[1], load.at[4]),
    ]
    for copy in loads:
        copy.start()

    barrier = pltpu.get_barrier_semaphore()
    peers = [at(k // 2, k % 2 == 1) for k in range(1, UNITS)] + [core_peer, y_peer]
    for peer in peers:
        pl.semaphore_signal(barrier, inc=1, device_id=peer, device_id_type=MESH)
    pl.semaphore_wait(barrier, len(peers))

    own_x(0).start()
    own_near(0).start()

    @pl.when(is_inner)
    def _():
        own_across(0).start()

    own_x(1).start()
    own_near(1).start()

    @pl.when(is_inner)
    def _():
        own_across(1).start()

    scores = gate[...]
    mix = scores * (ROUTE_SCALE / jnp.sum(scores, axis=0, keepdims=True))
    ids = route[...]
    named = lax.broadcasted_iota(jnp.int32, (UNITS, rows), 0)
    spread = jnp.zeros((UNITS, rows), F32)
    for k in range(UNITS):
        spread = spread + jnp.where(ids[k:k + 1, :] == named, mix[k:k + 1, :], 0.0)
    wt[0] = spread
    for k in range(1, UNITS):
        weight(k).start()
    for copy in loads:
        copy.wait()

    def first_arrivals():
        for p in range(2):
            token_in(1, p).wait_recv()

            @pl.when(is_inner)
            def _():
                near_across(p).start()
                token_in(3, p).wait_recv()
                across_near(p).start()
                second_x(p).start()

            if p == 1:
                near_x(1).start()
            token_in(2, p).wait_recv()

            if p == 0:
                @pl.when(jnp.logical_not(is_inner))
                def _():
                    side_near(0).start()

    def second_arrivals():
        for p in range(2):
            @pl.when(is_inner)
            def _():
                token_in(5, p).wait_recv()
                far_near(p).start()
                third_x(p).start()

            @pl.when(jnp.logical_not(is_inner))
            def _():
                token_in(3, p).wait_recv()
                second_x(p).start()

        @pl.when(is_inner)
        def _():
            side_near(0).start()

    def third_arrivals():
        for p in range(2):
            @pl.when(jnp.logical_not(is_inner))
            def _():
                token_in(5, p).wait_recv()
                third_x(p).start()

        token_in(4, 0).wait_recv()
        token_in(4, 1).wait_recv()

    def stage_a(u):
        @pl.when(u >= 6)
        def _():
            token_in(u, 0).wait_recv()
            token_in(u, 1).wait_recv()

        block = got[u]
        core_out[u] = jnp.dot(block, upv[1], preferred_element_type=F32).astype(BF16)
        core_copy(u).start()
        kept[u] = jnp.dot(block, upv[0], preferred_element_type=F32)

    def stage_b(u):
        core_copy(u).wait_recv()
        total = kept[u] + core_in[u].astype(F32)
        kept[u] = total
        y_out[u] = total.astype(BF16)
        y_copy(u).start()

    def stage_c(u):
        y_copy(u).wait_recv()
        before = kept[u] + y_in[u].astype(F32)
        hid[u, 0] = (before / (1.0 + jnp.exp(-before))).astype(BF16)
        hid_copy(u).start()

    def stage_d(u):
        other = (u == 2) | (u == 4) | (u >= 6)
        d = jnp.where((u == 1) | (u == 6), 1, jnp.where((u == 3) | (u == 4), second, third))
        d = jnp.where((u == 0) | (u == 2), 0, d)
        k = 2 * d + other.astype(jnp.int32)

        @pl.when(u >= 1)
        def _():
            weight_in(k).wait_recv()

        scale = jnp.broadcast_to(wt[k, pl.ds(expert, 1), :], (128, rows)).T
        hid_copy(u).wait_recv()
        result = jnp.dot(hid[u, 0], downv[0], preferred_element_type=F32)
        result = result + jnp.dot(hid[u, 1], downv[1], preferred_element_type=F32)
        result = result * jnp.concatenate([scale] * (result.shape[1] // 128), axis=1)

        @pl.when((u == 0) | (u == 3) | (u == 5))
        def _():
            acc[d] = result

        @pl.when(u == 1)
        def _():
            z_out[1] = result.astype(BF16)

            @pl.when(jnp.logical_not(is_inner))
            def _():
                z_copy(1, 0).start()
                z_copy(1, 1).start()

        @pl.when(u == 2)
        def _():
            over[0] = result.astype(BF16)

        @pl.when(u == 6)
        def _():
            over[1] = result.astype(BF16)
            over_copy(0).start()
            over_copy(1).start()

        @pl.when((u == 4) | (u == 7))
        def _():
            x_out[d] = result.astype(BF16)
            x_copy(d, 0).start()
            x_copy(d, 1).start()

    def stage_e(d, p):
        x_copy(d, p).wait_recv()
        z_out[d, lines(p)] = (acc[d, lines(p)] + x_in[d, lines(p)].astype(F32)).astype(BF16)
        z_copy(d, p).start()

    def step(t, carry):
        @pl.when(t == 3)
        def _():
            second_arrivals()

        @pl.when(t == 4)
        def _():
            third_arrivals()

        @pl.when(t < UNITS)
        def _():
            stage_a(t)

        @pl.when((t >= 2) & (t < UNITS + 1))
        def _():
            stage_b(t - 1)

        @pl.when((t >= 2) & (t < UNITS + 2))
        def _():
            stage_c(t - 2)

        @pl.when((t >= 3) & (t < UNITS + 3))
        def _():
            stage_d(t - 3)

        @pl.when((t == 7) & is_inner)
        def _():
            z_copy(1, 0).start()
            z_copy(1, 1).start()

        @pl.when(t == 8)
        def _():
            stage_e(second, 0)
            stage_e(second, 1)

        return carry

    stage_a(0)
    stage_b(0)
    first_arrivals()
    lax.fori_loop(1, UNITS + 3, step, 0)

    for p in range(2):
        for copy in (own_x, own_near, second_x, third_x):
            copy(p).wait_send()
    side_near(0).wait_send()
    near_x(1).wait_send()

    @pl.when(is_inner)
    def _():
        for p in range(2):
            for copy in (own_across, near_across, far_near, across_near):
                copy(p).wait_send()

    for u in range(UNITS):
        if u:
            weight(u).wait_send()
        core_copy(u).wait_send()
        y_copy(u).wait_send()
        hid_copy(u).wait_send()

    for p in range(2):
        stage_e(third, p)
        over_copy(p).wait_recv()
        x_out[0, lines(p)] = (over[0, lines(p)].astype(F32) + over[2, lines(p)].astype(F32)).astype(BF16)
        x_copy(0, p).start()

    for p in range(2):
        over_copy(p).wait_send()
        x_copy(2, p).wait_send()
        x_copy(3, p).wait_send()
        for d in range(1, NZ):
            z_copy(d, p).wait_send()

    for p in range(2):
        total = acc[0, lines(p)]
        for d in range(1, NZ):
            z_copy(d, p).wait_recv()
            total = total + z_in[d, lines(p)].astype(F32)
        x_copy(0, p).wait_recv()
        out[lines(p)] = (total + x_in[0, lines(p)].astype(F32)).astype(BF16)
    for p in range(2):
        x_copy(0, p).wait_send()


def dense(tokens, route_ids, gate_scores, up_weight, down_weight):
    rows, features = tokens.shape
    hidden = up_weight.shape[2]
    half = hidden // 2
    vmem = pl.BlockSpec(memory_space=pltpu.VMEM)
    hbm = pl.BlockSpec(memory_space=pltpu.HBM)
    dma = pltpu.SemaphoreType.DMA
    return pl.pallas_call(
        dense_kernel,
        out_shape=jax.ShapeDtypeStruct((rows, features), BF16),
        in_specs=[hbm, vmem, vmem, hbm, hbm],
        out_specs=vmem,
        scratch_shapes=[
            pltpu.VMEM((UNITS, rows, features), BF16),
            pltpu.VMEM((2, features, half), BF16),
            pltpu.VMEM((2, half, features), BF16),
            pltpu.VMEM((UNITS, UNITS, rows), F32),
            pltpu.VMEM((UNITS, rows, half), BF16),
            pltpu.VMEM((UNITS, rows, half), BF16),
            pltpu.VMEM((UNITS, rows, half), F32),
            pltpu.VMEM((UNITS, rows, half), BF16),
            pltpu.VMEM((UNITS, rows, half), BF16),
            pltpu.VMEM((UNITS, 2, rows, half), BF16),
            pltpu.VMEM((NZ, rows, features), F32),
            pltpu.VMEM((3, rows, features), BF16),
            pltpu.VMEM((NZ, rows, features), BF16),
            pltpu.VMEM((NZ, rows, features), BF16),
            pltpu.VMEM((NZ, rows, features), BF16),
            pltpu.VMEM((NZ, rows, features), BF16),
        ] + [dma((10, 2)), dma((UNITS, 2))] + [dma((UNITS,))] * 8 + [dma((NZ, 2))] * 4 + [dma((5,))],
        compiler_params=pltpu.CompilerParams(
            collective_id=0, has_side_effects=True, vmem_limit_bytes=63 * 2**20
        ),
        cost_estimate=pl.CostEstimate(
            flops=4 * UNITS * rows * features * hidden,
            bytes_accessed=4 * features * hidden + 4 * rows * features,
            transcendentals=UNITS * rows * half,
        ),
    )(tokens, route_ids.T, gate_scores.T, up_weight, down_weight)


def local(tokens, route_ids, gate_scores, up_weight, down_weight):
    experts = lax.axis_size("expert")
    every = route_ids.shape[1] == experts == UNITS and lax.axis_size("dp") == 4
    body = dense if every and tokens.shape[0] == 128 else routed
    return body(tokens, route_ids, gate_scores, up_weight, down_weight)


def solution(mesh):
    return jax.shard_map(
        local,
        mesh=mesh,
        in_specs=(
            P("expert", "dp"),
            P("expert", None),
            P("expert", None),
            P("expert", "dp", None),
            P("expert", None, "dp"),
        ),
        out_specs=P("expert", "dp"),
        check_vma=False,
    )
```

```python
import functools

import jax
import jax.numpy as jnp
from jax import lax
from jax.experimental import pallas as pl
from jax.experimental.pallas import tpu as pltpu
from jax.sharding import PartitionSpec as P

HOT = 2


ROUTE_SCALE = 2.5


def silu_hidden(before):
    summed = lax.psum(before.astype(jnp.bfloat16), "dp").astype(jnp.float32)
    result = jax.nn.silu(summed).astype(jnp.bfloat16)
    return result


def routed(tokens, route_ids, gate_scores, up_weight, down_weight):
    token_count, chosen_count = route_ids.shape
    features = tokens.shape[1]
    experts = lax.axis_size("expert")
    mean_rows = token_count * chosen_count // experts
    hot_most = min(2 * mean_rows - 1, token_count)
    cold_rows = (experts - HOT) * mean_rows - HOT * (hot_most - mean_rows)
    cold_most = -(-cold_rows // (experts - HOT))
    flat_ids = route_ids.reshape(-1)
    row_total = flat_ids.shape[0]
    expert_range = jnp.arange(experts, dtype=jnp.int32)
    onehot = (flat_ids[:, None] == expert_range[None, :]).astype(jnp.int32)
    running = jnp.cumsum(onehot, axis=0) - 1
    row_ranks = jnp.sum(onehot * running, axis=1)
    padded = jnp.concatenate([tokens, jnp.zeros((1, features), tokens.dtype)], axis=0)
    up_local = up_weight[0]
    down_local = down_weight[0]
    mix_weights = gate_scores * (ROUTE_SCALE / jnp.sum(gate_scores, axis=1, keepdims=True))
    slot_count = max(hot_most, cold_most)
    slot_of_row = flat_ids * slot_count + row_ranks
    slot_table = jnp.full((experts * slot_count,), row_total, jnp.int32)
    slot_table = slot_table.at[slot_of_row].set(jnp.arange(row_total, dtype=jnp.int32), mode="drop")
    sending = padded[slot_table // chosen_count].reshape(experts, slot_count, features)
    arrived = lax.all_to_all(sending, "expert", split_axis=0, concat_axis=0, tiled=True)
    item_count = arrived.shape[1]
    flat_rows = arrived.reshape(-1, features)
    before = jnp.dot(flat_rows, up_local, preferred_element_type=jnp.float32)
    hidden = silu_hidden(before)
    output = jnp.dot(hidden, down_local, preferred_element_type=jnp.float32)
    outcome = output.astype(jnp.bfloat16).reshape(experts, item_count, features)
    returned = lax.all_to_all(outcome, "expert", split_axis=0, concat_axis=0, tiled=True).reshape(
        -1, features
    )
    picked = returned[slot_of_row]
    picked = picked.reshape(token_count, chosen_count, features).astype(jnp.float32)
    mixed = jnp.sum(mix_weights[:, :, None] * picked, axis=1)
    return mixed.astype(jnp.bfloat16)


MESH = pl.DeviceIdType.MESH
F32 = jnp.float32
BF16 = jnp.bfloat16
NZ, NX = 4, 2
UNITS = NZ * NX


def mesh_xor(z, d):
    high = lax.rem(lax.div(z, 2) + lax.div(d, 2), 2)
    low = lax.rem(lax.rem(z, 2) + lax.rem(d, 2), 2)
    return high * 2 + low


def dense_kernel(
    tokens, route, gate, up, down, out,
    got, upv, downv, wt, core_out, core_in, kept, y_out, y_in, hid, acc, over, x_out, x_in, z_out, z_in,
    tok_s, tok_r, w_s, w_r, core_s, core_r, y_s, y_r, hid_s, hid_r, x_s, x_r, z_s, z_r, load,
):
    expert = lax.axis_index("expert")
    part = lax.axis_index("dp")
    z, x = lax.div(expert, NX), lax.rem(expert, NX)
    y, core = lax.div(part, 2), lax.rem(part, 2)
    half = upv.shape[2]
    rows = tokens.shape[0]

    def at(d, other):
        xx = 1 - x if other else x
        return {"expert": mesh_xor(z, d) * NX + xx}

    x_peer = {"expert": z * NX + 1 - x}
    core_peer = {"dp": y * 2 + 1 - core}
    y_peer = {"dp": (1 - y) * 2 + core}

    def remote(src, dst, send, recv, device):
        return pltpu.make_async_remote_copy(
            src_ref=src, dst_ref=dst, send_sem=send, recv_sem=recv,
            device_id=device, device_id_type=MESH,
        )

    inner = lax.rem(mesh_xor(z, lax.div(z, 2)), 2)
    is_inner = inner == 1
    near, across = at(1, False), at(3, False)

    def token(k, src, slot, device):
        def piece(p):
            return remote(
                src.at[lines(p)], got.at[slot, lines(p)], tok_s.at[k, p], tok_r.at[slot, p], device)
        return piece

    def token_in(u, p):
        return remote(tokens.at[lines(p)], got.at[u, lines(p)], tok_s.at[0, p], tok_r.at[u, p], x_peer)

    second, third = 2 + inner, 3 - inner
    own_x = token(0, tokens, 2, x_peer)
    own_near = token(1, tokens, 1, near)
    own_across = token(2, tokens, 3, across)
    near_across = token(3, got.at[1], 5, across)
    side_near = token(4, got.at[2], 6, near)
    across_near = token(5, got.at[3], 3, near)
    far_near = token(6, got.at[5], 5, near)
    second_x = token(7, got.at[3], 4, x_peer)
    third_x = token(8, got.at[5], 7, x_peer)
    near_x = token(9, got.at[1], 6, x_peer)

    def weight(k):
        return remote(wt.at[0], wt.at[k], w_s.at[k], w_r.at[k], at(k // 2, k % 2 == 1))

    def weight_in(u):
        return remote(wt.at[0], wt.at[u], w_s.at[u], w_r.at[u], x_peer)

    def core_copy(u):
        return remote(core_out.at[u], core_in.at[u], core_s.at[u], core_r.at[u], core_peer)

    def y_copy(u):
        return remote(y_out.at[u], y_in.at[u], y_s.at[u], y_r.at[u], y_peer)

    def hid_copy(u):
        return remote(hid.at[u, 0], hid.at[u, 1], hid_s.at[u], hid_r.at[u], core_peer)

    part_rows = rows // 2

    def lines(p):
        return pl.ds(p * part_rows, part_rows)

    def x_copy(d, p):
        return remote(x_out.at[d, lines(p)], x_in.at[d, lines(p)], x_s.at[d, p], x_r.at[d, p], x_peer)

    def over_copy(p):
        return remote(over.at[1, lines(p)], over.at[2, lines(p)], z_s.at[0, p], z_r.at[0, p], near)

    def z_copy(d, p):
        return remote(z_out.at[d, lines(p)], z_in.at[d, lines(p)], z_s.at[d, p], z_r.at[d, p], at(d, False))

    own = pl.ds(pl.multiple_of(core * half, half), half)
    theirs = pl.ds(pl.multiple_of((1 - core) * half, half), half)
    loads = [
        pltpu.make_async_copy(tokens, got.at[0], load.at[0]),
        pltpu.make_async_copy(up.at[0, :, theirs], upv.at[1], load.at[1]),
        pltpu.make_async_copy(up.at[0, :, own], upv.at[0], load.at[2]),
        pltpu.make_async_copy(down.at[0, own, :], downv.at[0], load.at[3]),
        pltpu.make_async_copy(down.at[0, theirs, :], downv.at[1], load.at[4]),
    ]
    for copy in loads:
        copy.start()

    barrier = pltpu.get_barrier_semaphore()
    peers = [at(k // 2, k % 2 == 1) for k in range(1, UNITS)] + [core_peer, y_peer]
    for peer in peers:
        pl.semaphore_signal(barrier, inc=1, device_id=peer, device_id_type=MESH)
    pl.semaphore_wait(barrier, len(peers))

    own_x(0).start()
    own_near(0).start()

    @pl.when(is_inner)
    def _():
        own_across(0).start()

    own_x(1).start()
    own_near(1).start()

    @pl.when(is_inner)
    def _():
        own_across(1).start()

    scores = gate[...]
    mix = scores * (ROUTE_SCALE / jnp.sum(scores, axis=0, keepdims=True))
    ids = route[...]
    named = lax.broadcasted_iota(jnp.int32, (UNITS, rows), 0)
    spread = jnp.zeros((UNITS, rows), F32)
    for k in range(UNITS):
        spread = spread + jnp.where(ids[k:k + 1, :] == named, mix[k:k + 1, :], 0.0)
    wt[0] = spread
    for k in range(1, UNITS):
        weight(k).start()
    for copy in loads:
        copy.wait()

    def first_arrivals():
        for p in range(2):
            token_in(1, p).wait_recv()

            @pl.when(is_inner)
            def _():
                near_across(p).start()
                token_in(3, p).wait_recv()
                across_near(p).start()
                second_x(p).start()

            if p == 1:
                near_x(1).start()
            token_in(2, p).wait_recv()

            if p == 0:
                @pl.when(jnp.logical_not(is_inner))
                def _():
                    side_near(0).start()

    def second_arrivals():
        for p in range(2):
            @pl.when(is_inner)
            def _():
                token_in(5, p).wait_recv()
                far_near(p).start()
                third_x(p).start()

            @pl.when(jnp.logical_not(is_inner))
            def _():
                token_in(3, p).wait_recv()
                second_x(p).start()

        @pl.when(is_inner)
        def _():
            side_near(0).start()

    def third_arrivals():
        for p in range(2):
            @pl.when(jnp.logical_not(is_inner))
            def _():
                token_in(5, p).wait_recv()
                third_x(p).start()

        token_in(4, 0).wait_recv()
        token_in(4, 1).wait_recv()

    def stage_a(u):
        @pl.when(u >= 6)
        def _():
            token_in(u, 0).wait_recv()
            token_in(u, 1).wait_recv()

        block = got[u]
        core_out[u] = jnp.dot(block, upv[1], preferred_element_type=F32).astype(BF16)
        core_copy(u).start()
        kept[u] = jnp.dot(block, upv[0], preferred_element_type=F32)

    def stage_b(u):
        core_copy(u).wait_recv()
        total = kept[u] + core_in[u].astype(F32)
        kept[u] = total
        y_out[u] = total.astype(BF16)
        y_copy(u).start()

    def stage_c(u):
        y_copy(u).wait_recv()
        before = kept[u] + y_in[u].astype(F32)
        hid[u, 0] = (before / (1.0 + jnp.exp(-before))).astype(BF16)
        hid_copy(u).start()

    def stage_d(u):
        other = (u == 2) | (u == 4) | (u >= 6)
        d = jnp.where((u == 1) | (u == 6), 1, jnp.where((u == 3) | (u == 4), second, third))
        d = jnp.where((u == 0) | (u == 2), 0, d)
        k = 2 * d + other.astype(jnp.int32)

        @pl.when(u >= 1)
        def _():
            weight_in(k).wait_recv()

        scale = jnp.broadcast_to(wt[k, pl.ds(expert, 1), :], (128, rows)).T
        hid_copy(u).wait_recv()
        result = jnp.dot(hid[u, 0], downv[0], preferred_element_type=F32)
        result = result + jnp.dot(hid[u, 1], downv[1], preferred_element_type=F32)
        result = result * jnp.concatenate([scale] * (result.shape[1] // 128), axis=1)

        @pl.when((u == 0) | (u == 3) | (u == 5))
        def _():
            acc[d] = result

        @pl.when(u == 1)
        def _():
            z_out[1] = result.astype(BF16)

            @pl.when(jnp.logical_not(is_inner))
            def _():
                z_copy(1, 0).start()
                z_copy(1, 1).start()

        @pl.when(u == 2)
        def _():
            over[0] = result.astype(BF16)

        @pl.when(u == 6)
        def _():
            over[1] = result.astype(BF16)
            over_copy(0).start()
            over_copy(1).start()

        @pl.when((u == 4) | (u == 7))
        def _():
            x_out[d] = result.astype(BF16)
            x_copy(d, 0).start()
            x_copy(d, 1).start()

    def stage_e(d, p):
        x_copy(d, p).wait_recv()
        z_out[d, lines(p)] = (acc[d, lines(p)] + x_in[d, lines(p)].astype(F32)).astype(BF16)
        z_copy(d, p).start()

    def step(t, carry):
        @pl.when(t == 3)
        def _():
            second_arrivals()

        @pl.when(t == 4)
        def _():
            third_arrivals()

        @pl.when(t < UNITS)
        def _():
            stage_a(t)

        @pl.when((t >= 2) & (t < UNITS + 1))
        def _():
            stage_b(t - 1)

        @pl.when((t >= 3) & (t < UNITS + 3))
        def _():
            stage_d(t - 3)

        @pl.when((t >= 2) & (t < UNITS + 2))
        def _():
            stage_c(t - 2)

        @pl.when((t == 7) & is_inner)
        def _():
            z_copy(1, 0).start()
            z_copy(1, 1).start()

        @pl.when(t == 8)
        def _():
            stage_e(second, 0)
            stage_e(second, 1)

        return carry

    stage_a(0)
    stage_b(0)
    first_arrivals()
    lax.fori_loop(1, UNITS + 3, step, 0)

    for p in range(2):
        for copy in (own_x, own_near, second_x, third_x):
            copy(p).wait_send()
    side_near(0).wait_send()
    near_x(1).wait_send()

    @pl.when(is_inner)
    def _():
        for p in range(2):
            for copy in (own_across, near_across, far_near, across_near):
                copy(p).wait_send()

    for u in range(UNITS):
        if u:
            weight(u).wait_send()
        core_copy(u).wait_send()
        y_copy(u).wait_send()
        hid_copy(u).wait_send()

    for p in range(2):
        stage_e(third, p)
        over_copy(p).wait_recv()
        x_out[0, lines(p)] = (over[0, lines(p)].astype(F32) + over[2, lines(p)].astype(F32)).astype(BF16)
        x_copy(0, p).start()

    for p in range(2):
        over_copy(p).wait_send()
        x_copy(2, p).wait_send()
        x_copy(3, p).wait_send()
        for d in range(1, NZ):
            z_copy(d, p).wait_send()

    for p in range(2):
        total = acc[0, lines(p)]
        for d in range(1, NZ):
            z_copy(d, p).wait_recv()
            total = total + z_in[d, lines(p)].astype(F32)
        x_copy(0, p).wait_recv()
        out[lines(p)] = (total + x_in[0, lines(p)].astype(F32)).astype(BF16)
    for p in range(2):
        x_copy(0, p).wait_send()


def dense(tokens, route_ids, gate_scores, up_weight, down_weight):
    rows, features = tokens.shape
    hidden = up_weight.shape[2]
    half = hidden // 2
    vmem = pl.BlockSpec(memory_space=pltpu.VMEM)
    hbm = pl.BlockSpec(memory_space=pltpu.HBM)
    dma = pltpu.SemaphoreType.DMA
    return pl.pallas_call(
        dense_kernel,
        out_shape=jax.ShapeDtypeStruct((rows, features), BF16),
        in_specs=[hbm, vmem, vmem, hbm, hbm],
        out_specs=vmem,
        scratch_shapes=[
            pltpu.VMEM((UNITS, rows, features), BF16),
            pltpu.VMEM((2, features, half), BF16),
            pltpu.VMEM((2, half, features), BF16),
            pltpu.VMEM((UNITS, UNITS, rows), F32),
            pltpu.VMEM((UNITS, rows, half), BF16),
            pltpu.VMEM((UNITS, rows, half), BF16),
            pltpu.VMEM((UNITS, rows, half), F32),
            pltpu.VMEM((UNITS, rows, half), BF16),
            pltpu.VMEM((UNITS, rows, half), BF16),
            pltpu.VMEM((UNITS, 2, rows, half), BF16),
            pltpu.VMEM((NZ, rows, features), F32),
            pltpu.VMEM((3, rows, features), BF16),
            pltpu.VMEM((NZ, rows, features), BF16),
            pltpu.VMEM((NZ, rows, features), BF16),
            pltpu.VMEM((NZ, rows, features), BF16),
            pltpu.VMEM((NZ, rows, features), BF16),
        ] + [dma((10, 2)), dma((UNITS, 2))] + [dma((UNITS,))] * 8 + [dma((NZ, 2))] * 4 + [dma((5,))],
        compiler_params=pltpu.CompilerParams(
            collective_id=0, has_side_effects=True, vmem_limit_bytes=63 * 2**20
        ),
        cost_estimate=pl.CostEstimate(
            flops=4 * UNITS * rows * features * hidden,
            bytes_accessed=4 * features * hidden + 4 * rows * features,
            transcendentals=UNITS * rows * half,
        ),
    )(tokens, route_ids.T, gate_scores.T, up_weight, down_weight)


def local(tokens, route_ids, gate_scores, up_weight, down_weight):
    experts = lax.axis_size("expert")
    every = route_ids.shape[1] == experts == UNITS and lax.axis_size("dp") == 4
    body = dense if every and tokens.shape[0] == 128 else routed
    return body(tokens, route_ids, gate_scores, up_weight, down_weight)


def solution(mesh):
    return jax.shard_map(
        local,
        mesh=mesh,
        in_specs=(
            P("expert", "dp"),
            P("expert", None),
            P("expert", None),
            P("expert", "dp", None),
            P("expert", None, "dp"),
        ),
        out_specs=P("expert", "dp"),
        check_vma=False,
    )
```

```python
import functools

import jax
import jax.numpy as jnp
from jax import lax
from jax.experimental import pallas as pl
from jax.experimental.pallas import tpu as pltpu
from jax.sharding import PartitionSpec as P

HOT = 2


ROUTE_SCALE = 2.5


def silu_hidden(before):
    summed = lax.psum(before.astype(jnp.bfloat16), "dp").astype(jnp.float32)
    result = jax.nn.silu(summed).astype(jnp.bfloat16)
    return result


def routed(tokens, route_ids, gate_scores, up_weight, down_weight):
    token_count, chosen_count = route_ids.shape
    features = tokens.shape[1]
    experts = lax.axis_size("expert")
    mean_rows = token_count * chosen_count // experts
    hot_most = min(2 * mean_rows - 1, token_count)
    cold_rows = (experts - HOT) * mean_rows - HOT * (hot_most - mean_rows)
    cold_most = -(-cold_rows // (experts - HOT))
    flat_ids = route_ids.reshape(-1)
    row_total = flat_ids.shape[0]
    expert_range = jnp.arange(experts, dtype=jnp.int32)
    onehot = (flat_ids[:, None] == expert_range[None, :]).astype(jnp.int32)
    running = jnp.cumsum(onehot, axis=0) - 1
    row_ranks = jnp.sum(onehot * running, axis=1)
    padded = jnp.concatenate([tokens, jnp.zeros((1, features), tokens.dtype)], axis=0)
    up_local = up_weight[0]
    down_local = down_weight[0]
    mix_weights = gate_scores * (ROUTE_SCALE / jnp.sum(gate_scores, axis=1, keepdims=True))
    slot_count = max(hot_most, cold_most)
    slot_of_row = flat_ids * slot_count + row_ranks
    slot_table = jnp.full((experts * slot_count,), row_total, jnp.int32)
    slot_table = slot_table.at[slot_of_row].set(jnp.arange(row_total, dtype=jnp.int32), mode="drop")
    sending = padded[slot_table // chosen_count].reshape(experts, slot_count, features)
    arrived = lax.all_to_all(sending, "expert", split_axis=0, concat_axis=0, tiled=True)
    item_count = arrived.shape[1]
    flat_rows = arrived.reshape(-1, features)
    before = jnp.dot(flat_rows, up_local, preferred_element_type=jnp.float32)
    hidden = silu_hidden(before)
    output = jnp.dot(hidden, down_local, preferred_element_type=jnp.float32)
    outcome = output.astype(jnp.bfloat16).reshape(experts, item_count, features)
    returned = lax.all_to_all(outcome, "expert", split_axis=0, concat_axis=0, tiled=True).reshape(
        -1, features
    )
    picked = returned[slot_of_row]
    picked = picked.reshape(token_count, chosen_count, features).astype(jnp.float32)
    mixed = jnp.sum(mix_weights[:, :, None] * picked, axis=1)
    return mixed.astype(jnp.bfloat16)


MESH = pl.DeviceIdType.MESH
F32 = jnp.float32
BF16 = jnp.bfloat16
NZ, NX = 4, 2
UNITS = NZ * NX


def mesh_xor(z, d):
    high = lax.rem(lax.div(z, 2) + lax.div(d, 2), 2)
    low = lax.rem(lax.rem(z, 2) + lax.rem(d, 2), 2)
    return high * 2 + low


def dense_kernel(
    tokens, route, gate, up, down, out,
    got, upv, downv, wt, core_out, core_in, kept, y_out, y_in, hid, acc, over, x_out, x_in, z_out, z_in,
    tok_s, tok_r, w_s, w_r, core_s, core_r, y_s, y_r, hid_s, hid_r, x_s, x_r, z_s, z_r, load,
):
    expert = lax.axis_index("expert")
    part = lax.axis_index("dp")
    z, x = lax.div(expert, NX), lax.rem(expert, NX)
    y, core = lax.div(part, 2), lax.rem(part, 2)
    half = upv.shape[2]
    rows = tokens.shape[0]

    def at(d, other):
        xx = 1 - x if other else x
        return {"expert": mesh_xor(z, d) * NX + xx}

    x_peer = {"expert": z * NX + 1 - x}
    core_peer = {"dp": y * 2 + 1 - core}
    y_peer = {"dp": (1 - y) * 2 + core}

    def remote(src, dst, send, recv, device):
        return pltpu.make_async_remote_copy(
            src_ref=src, dst_ref=dst, send_sem=send, recv_sem=recv,
            device_id=device, device_id_type=MESH,
        )

    inner = lax.rem(mesh_xor(z, lax.div(z, 2)), 2)
    is_inner = inner == 1
    near, across = at(1, False), at(3, False)

    def token(k, src, slot, device):
        def piece(p):
            return remote(
                src.at[lines(p)], got.at[slot, lines(p)], tok_s.at[k, p], tok_r.at[slot, p], device)
        return piece

    def token_in(u, p):
        return remote(tokens.at[lines(p)], got.at[u, lines(p)], tok_s.at[0, p], tok_r.at[u, p], x_peer)

    second, third = 2 + inner, 3 - inner
    own_x = token(0, tokens, 2, x_peer)
    own_near = token(1, tokens, 1, near)
    own_across = token(2, tokens, 3, across)
    near_across = token(3, got.at[1], 5, across)
    side_near = token(4, got.at[2], 6, near)
    across_near = token(5, got.at[3], 3, near)
    far_near = token(6, got.at[5], 5, near)
    second_x = token(7, got.at[3], 4, x_peer)
    third_x = token(8, got.at[5], 7, x_peer)
    near_x = token(9, got.at[1], 6, x_peer)

    def weight(k):
        return remote(wt.at[0], wt.at[k], w_s.at[k], w_r.at[k], at(k // 2, k % 2 == 1))

    def weight_in(u):
        return remote(wt.at[0], wt.at[u], w_s.at[u], w_r.at[u], x_peer)

    def core_copy(u):
        return remote(core_out.at[u], core_in.at[u], core_s.at[u], core_r.at[u], core_peer)

    def y_copy(u):
        return remote(y_out.at[u], y_in.at[u], y_s.at[u], y_r.at[u], y_peer)

    def hid_copy(u):
        return remote(hid.at[u, :, :half], hid.at[u, :, half:], hid_s.at[u], hid_r.at[u], core_peer)

    part_rows = rows // 2

    def lines(p):
        return pl.ds(p * part_rows, part_rows)

    def x_copy(d, p):
        return remote(x_out.at[d, lines(p)], x_in.at[d, lines(p)], x_s.at[d, p], x_r.at[d, p], x_peer)

    def over_copy(p):
        return remote(over.at[1, lines(p)], over.at[2, lines(p)], z_s.at[0, p], z_r.at[0, p], near)

    def z_copy(d, p):
        return remote(z_out.at[d, lines(p)], z_in.at[d, lines(p)], z_s.at[d, p], z_r.at[d, p], at(d, False))

    own = pl.ds(pl.multiple_of(core * half, half), half)
    theirs = pl.ds(pl.multiple_of((1 - core) * half, half), half)
    loads = [
        pltpu.make_async_copy(tokens, got.at[0], load.at[0]),
        pltpu.make_async_copy(up.at[0, :, theirs], upv.at[1], load.at[1]),
        pltpu.make_async_copy(up.at[0, :, own], upv.at[0], load.at[2]),
        pltpu.make_async_copy(down.at[0, own, :], downv.at[:half], load.at[3]),
        pltpu.make_async_copy(down.at[0, theirs, :], downv.at[half:], load.at[4]),
    ]
    for copy in loads:
        copy.start()

    barrier = pltpu.get_barrier_semaphore()
    peers = [at(k // 2, k % 2 == 1) for k in range(1, UNITS)] + [core_peer, y_peer]
    for peer in peers:
        pl.semaphore_signal(barrier, inc=1, device_id=peer, device_id_type=MESH)
    pl.semaphore_wait(barrier, len(peers))

    own_x(0).start()
    own_near(0).start()

    @pl.when(is_inner)
    def _():
        own_across(0).start()

    own_x(1).start()
    own_near(1).start()

    @pl.when(is_inner)
    def _():
        own_across(1).start()

    scores = gate[...]
    mix = scores * (ROUTE_SCALE / jnp.sum(scores, axis=0, keepdims=True))
    ids = route[...]
    named = lax.broadcasted_iota(jnp.int32, (UNITS, rows), 0)
    spread = jnp.zeros((UNITS, rows), F32)
    for k in range(UNITS):
        spread = spread + jnp.where(ids[k:k + 1, :] == named, mix[k:k + 1, :], 0.0)
    wt[0] = spread
    for k in range(1, UNITS):
        weight(k).start()
    for copy in loads:
        copy.wait()

    def first_arrivals():
        for p in range(2):
            token_in(1, p).wait_recv()

            @pl.when(is_inner)
            def _():
                near_across(p).start()
                token_in(3, p).wait_recv()
                across_near(p).start()
                second_x(p).start()

            if p == 1:
                near_x(1).start()
            token_in(2, p).wait_recv()

            if p == 0:
                @pl.when(jnp.logical_not(is_inner))
                def _():
                    side_near(0).start()

    def second_arrivals():
        for p in range(2):
            @pl.when(is_inner)
            def _():
                token_in(5, p).wait_recv()
                far_near(p).start()
                third_x(p).start()

            @pl.when(jnp.logical_not(is_inner))
            def _():
                token_in(3, p).wait_recv()
                second_x(p).start()

        @pl.when(is_inner)
        def _():
            side_near(0).start()

    def third_arrivals():
        for p in range(2):
            @pl.when(jnp.logical_not(is_inner))
            def _():
                token_in(5, p).wait_recv()
                third_x(p).start()

        token_in(4, 0).wait_recv()
        token_in(4, 1).wait_recv()

    def stage_a(u):
        @pl.when(u >= 6)
        def _():
            token_in(u, 0).wait_recv()
            token_in(u, 1).wait_recv()

        block = got[u]
        core_out[u] = jnp.dot(block, upv[1], preferred_element_type=F32).astype(BF16)
        core_copy(u).start()
        kept[u] = jnp.dot(block, upv[0], preferred_element_type=F32)

    def stage_b(u):
        core_copy(u).wait_recv()
        total = kept[u] + core_in[u].astype(F32)
        kept[u] = total
        y_out[u] = total.astype(BF16)
        y_copy(u).start()

    def stage_c(u):
        y_copy(u).wait_recv()
        before = kept[u] + y_in[u].astype(F32)
        hid[u, :, :half] = (before / (1.0 + jnp.exp(-before))).astype(BF16)
        hid_copy(u).start()

    def stage_d(u):
        other = (u == 2) | (u == 4) | (u >= 6)
        d = jnp.where((u == 1) | (u == 6), 1, jnp.where((u == 3) | (u == 4), second, third))
        d = jnp.where((u == 0) | (u == 2), 0, d)
        k = 2 * d + other.astype(jnp.int32)

        @pl.when(u >= 1)
        def _():
            weight_in(k).wait_recv()

        scale = jnp.broadcast_to(wt[k, pl.ds(expert, 1), :], (128, rows)).T
        hid_copy(u).wait_recv()
        result = jnp.dot(hid[u], downv[...], preferred_element_type=F32)
        result = result * jnp.concatenate([scale] * (result.shape[1] // 128), axis=1)

        @pl.when((u == 0) | (u == 3) | (u == 5))
        def _():
            acc[d] = result

        @pl.when(u == 1)
        def _():
            z_out[1] = result.astype(BF16)

            @pl.when(jnp.logical_not(is_inner))
            def _():
                z_copy(1, 0).start()
                z_copy(1, 1).start()

        @pl.when(u == 2)
        def _():
            over[0] = result.astype(BF16)

        @pl.when(u == 6)
        def _():
            over[1] = result.astype(BF16)
            over_copy(0).start()
            over_copy(1).start()

        @pl.when((u == 4) | (u == 7))
        def _():
            x_out[d] = result.astype(BF16)
            x_copy(d, 0).start()
            x_copy(d, 1).start()

    def stage_e(d, p):
        x_copy(d, p).wait_recv()
        z_out[d, lines(p)] = (acc[d, lines(p)] + x_in[d, lines(p)].astype(F32)).astype(BF16)
        z_copy(d, p).start()

    def step(t, carry):
        @pl.when(t == 3)
        def _():
            second_arrivals()

        @pl.when(t == 4)
        def _():
            third_arrivals()

        @pl.when(t < UNITS)
        def _():
            stage_a(t)

        @pl.when((t >= 2) & (t < UNITS + 1))
        def _():
            stage_b(t - 1)

        @pl.when((t >= 2) & (t < UNITS + 2))
        def _():
            stage_c(t - 2)

        @pl.when((t >= 3) & (t < UNITS + 3))
        def _():
            stage_d(t - 3)

        @pl.when((t == 7) & is_inner)
        def _():
            z_copy(1, 0).start()
            z_copy(1, 1).start()

        @pl.when(t == 8)
        def _():
            stage_e(second, 0)
            stage_e(second, 1)

        return carry

    stage_a(0)
    stage_b(0)
    first_arrivals()
    lax.fori_loop(1, UNITS + 3, step, 0)

    for p in range(2):
        for copy in (own_x, own_near, second_x, third_x):
            copy(p).wait_send()
    side_near(0).wait_send()
    near_x(1).wait_send()

    @pl.when(is_inner)
    def _():
        for p in range(2):
            for copy in (own_across, near_across, far_near, across_near):
                copy(p).wait_send()

    for u in range(UNITS):
        if u:
            weight(u).wait_send()
        core_copy(u).wait_send()
        y_copy(u).wait_send()
        hid_copy(u).wait_send()

    for p in range(2):
        stage_e(third, p)
        over_copy(p).wait_recv()
        x_out[0, lines(p)] = (over[0, lines(p)].astype(F32) + over[2, lines(p)].astype(F32)).astype(BF16)
        x_copy(0, p).start()

    for p in range(2):
        over_copy(p).wait_send()
        x_copy(2, p).wait_send()
        x_copy(3, p).wait_send()
        for d in range(1, NZ):
            z_copy(d, p).wait_send()

    for p in range(2):
        total = acc[0, lines(p)]
        for d in range(1, NZ):
            z_copy(d, p).wait_recv()
            total = total + z_in[d, lines(p)].astype(F32)
        x_copy(0, p).wait_recv()
        out[lines(p)] = (total + x_in[0, lines(p)].astype(F32)).astype(BF16)
    for p in range(2):
        x_copy(0, p).wait_send()


def dense(tokens, route_ids, gate_scores, up_weight, down_weight):
    rows, features = tokens.shape
    hidden = up_weight.shape[2]
    half = hidden // 2
    vmem = pl.BlockSpec(memory_space=pltpu.VMEM)
    hbm = pl.BlockSpec(memory_space=pltpu.HBM)
    dma = pltpu.SemaphoreType.DMA
    return pl.pallas_call(
        dense_kernel,
        out_shape=jax.ShapeDtypeStruct((rows, features), BF16),
        in_specs=[hbm, vmem, vmem, hbm, hbm],
        out_specs=vmem,
        scratch_shapes=[
            pltpu.VMEM((UNITS, rows, features), BF16),
            pltpu.VMEM((2, features, half), BF16),
            pltpu.VMEM((hidden, features), BF16),
            pltpu.VMEM((UNITS, UNITS, rows), F32),
            pltpu.VMEM((UNITS, rows, half), BF16),
            pltpu.VMEM((UNITS, rows, half), BF16),
            pltpu.VMEM((UNITS, rows, half), F32),
            pltpu.VMEM((UNITS, rows, half), BF16),
            pltpu.VMEM((UNITS, rows, half), BF16),
            pltpu.VMEM((UNITS, rows, hidden), BF16),
            pltpu.VMEM((NZ, rows, features), F32),
            pltpu.VMEM((3, rows, features), BF16),
            pltpu.VMEM((NZ, rows, features), BF16),
            pltpu.VMEM((NZ, rows, features), BF16),
            pltpu.VMEM((NZ, rows, features), BF16),
            pltpu.VMEM((NZ, rows, features), BF16),
        ] + [dma((10, 2)), dma((UNITS, 2))] + [dma((UNITS,))] * 8 + [dma((NZ, 2))] * 4 + [dma((5,))],
        compiler_params=pltpu.CompilerParams(
            collective_id=0, has_side_effects=True, vmem_limit_bytes=63 * 2**20
        ),
        cost_estimate=pl.CostEstimate(
            flops=4 * UNITS * rows * features * hidden,
            bytes_accessed=4 * features * hidden + 4 * rows * features,
            transcendentals=UNITS * rows * half,
        ),
    )(tokens, route_ids.T, gate_scores.T, up_weight, down_weight)


def local(tokens, route_ids, gate_scores, up_weight, down_weight):
    experts = lax.axis_size("expert")
    every = route_ids.shape[1] == experts == UNITS and lax.axis_size("dp") == 4
    body = dense if every and tokens.shape[0] == 128 else routed
    return body(tokens, route_ids, gate_scores, up_weight, down_weight)


def solution(mesh):
    return jax.shard_map(
        local,
        mesh=mesh,
        in_specs=(
            P("expert", "dp"),
            P("expert", None),
            P("expert", None),
            P("expert", "dp", None),
            P("expert", None, "dp"),
        ),
        out_specs=P("expert", "dp"),
        check_vma=False,
    )
```

```python
import functools

import jax
import jax.numpy as jnp
from jax import lax
from jax.experimental import pallas as pl
from jax.experimental.pallas import tpu as pltpu
from jax.sharding import PartitionSpec as P

HOT = 2


ROUTE_SCALE = 2.5


def silu_hidden(before):
    summed = lax.psum(before.astype(jnp.bfloat16), "dp").astype(jnp.float32)
    result = jax.nn.silu(summed).astype(jnp.bfloat16)
    return result


def routed(tokens, route_ids, gate_scores, up_weight, down_weight):
    token_count, chosen_count = route_ids.shape
    features = tokens.shape[1]
    experts = lax.axis_size("expert")
    mean_rows = token_count * chosen_count // experts
    hot_most = min(2 * mean_rows - 1, token_count)
    cold_rows = (experts - HOT) * mean_rows - HOT * (hot_most - mean_rows)
    cold_most = -(-cold_rows // (experts - HOT))
    flat_ids = route_ids.reshape(-1)
    row_total = flat_ids.shape[0]
    expert_range = jnp.arange(experts, dtype=jnp.int32)
    onehot = (flat_ids[:, None] == expert_range[None, :]).astype(jnp.int32)
    running = jnp.cumsum(onehot, axis=0) - 1
    row_ranks = jnp.sum(onehot * running, axis=1)
    padded = jnp.concatenate([tokens, jnp.zeros((1, features), tokens.dtype)], axis=0)
    up_local = up_weight[0]
    down_local = down_weight[0]
    mix_weights = gate_scores * (ROUTE_SCALE / jnp.sum(gate_scores, axis=1, keepdims=True))
    slot_count = max(hot_most, cold_most)
    slot_of_row = flat_ids * slot_count + row_ranks
    slot_table = jnp.full((experts * slot_count,), row_total, jnp.int32)
    slot_table = slot_table.at[slot_of_row].set(jnp.arange(row_total, dtype=jnp.int32), mode="drop")
    sending = padded[slot_table // chosen_count].reshape(experts, slot_count, features)
    arrived = lax.all_to_all(sending, "expert", split_axis=0, concat_axis=0, tiled=True)
    item_count = arrived.shape[1]
    flat_rows = arrived.reshape(-1, features)
    before = jnp.dot(flat_rows, up_local, preferred_element_type=jnp.float32)
    hidden = silu_hidden(before)
    output = jnp.dot(hidden, down_local, preferred_element_type=jnp.float32)
    outcome = output.astype(jnp.bfloat16).reshape(experts, item_count, features)
    returned = lax.all_to_all(outcome, "expert", split_axis=0, concat_axis=0, tiled=True).reshape(
        -1, features
    )
    picked = returned[slot_of_row]
    picked = picked.reshape(token_count, chosen_count, features).astype(jnp.float32)
    mixed = jnp.sum(mix_weights[:, :, None] * picked, axis=1)
    return mixed.astype(jnp.bfloat16)


MESH = pl.DeviceIdType.MESH
F32 = jnp.float32
BF16 = jnp.bfloat16
NZ, NX = 4, 2
UNITS = NZ * NX


def mesh_xor(z, d):
    high = lax.rem(lax.div(z, 2) + lax.div(d, 2), 2)
    low = lax.rem(lax.rem(z, 2) + lax.rem(d, 2), 2)
    return high * 2 + low


def dense_kernel(
    tokens, route, gate, up, down, out,
    got, upv, downv, wt, core_out, core_in, kept, y_out, y_in, hid, acc, over, x_out, x_in, z_out, z_in,
    tok_s, tok_r, w_s, w_r, core_s, core_r, y_s, y_r, hid_s, hid_r, x_s, x_r, z_s, z_r, load,
):
    expert = lax.axis_index("expert")
    part = lax.axis_index("dp")
    z, x = lax.div(expert, NX), lax.rem(expert, NX)
    y, core = lax.div(part, 2), lax.rem(part, 2)
    half = upv.shape[2]
    rows = tokens.shape[0]

    def at(d, other):
        xx = 1 - x if other else x
        return {"expert": mesh_xor(z, d) * NX + xx}

    x_peer = {"expert": z * NX + 1 - x}
    core_peer = {"dp": y * 2 + 1 - core}
    y_peer = {"dp": (1 - y) * 2 + core}

    def remote(src, dst, send, recv, device):
        return pltpu.make_async_remote_copy(
            src_ref=src, dst_ref=dst, send_sem=send, recv_sem=recv,
            device_id=device, device_id_type=MESH,
        )

    inner = lax.rem(mesh_xor(z, lax.div(z, 2)), 2)
    is_inner = inner == 1
    near, across = at(1, False), at(3, False)

    def token(k, src, slot, device):
        def piece(p):
            return remote(
                src.at[lines(p)], got.at[slot, lines(p)], tok_s.at[k, p], tok_r.at[slot, p], device)
        return piece

    def token_in(u, p):
        return remote(tokens.at[lines(p)], got.at[u, lines(p)], tok_s.at[0, p], tok_r.at[u, p], x_peer)

    second, third = 2 + inner, 3 - inner
    own_x = token(0, tokens, 2, x_peer)
    own_near = token(1, tokens, 1, near)
    own_across = token(2, tokens, 3, across)
    near_across = token(3, got.at[1], 6, across)
    side_near = token(4, got.at[2], 5, near)
    across_near = token(5, got.at[3], 3, near)
    far_near = token(6, got.at[6], 6, near)
    second_x = token(7, got.at[3], 4, x_peer)
    third_x = token(8, got.at[6], 7, x_peer)
    near_x = token(9, got.at[1], 5, x_peer)

    def weight(k):
        return remote(wt.at[0], wt.at[k], w_s.at[k], w_r.at[k], at(k // 2, k % 2 == 1))

    def weight_in(u):
        return remote(wt.at[0], wt.at[u], w_s.at[u], w_r.at[u], x_peer)

    def core_copy(u):
        return remote(core_out.at[u], core_in.at[u], core_s.at[u], core_r.at[u], core_peer)

    def y_copy(u):
        return remote(y_out.at[u], y_in.at[u], y_s.at[u], y_r.at[u], y_peer)

    def hid_copy(u):
        return remote(hid.at[u, :, :half], hid.at[u, :, half:], hid_s.at[u], hid_r.at[u], core_peer)

    part_rows = rows // 2

    def lines(p):
        return pl.ds(p * part_rows, part_rows)

    def x_copy(d, p):
        return remote(x_out.at[d, lines(p)], x_in.at[d, lines(p)], x_s.at[d, p], x_r.at[d, p], x_peer)

    def over_copy(p):
        return remote(over.at[1, lines(p)], over.at[2, lines(p)], z_s.at[0, p], z_r.at[0, p], near)

    def z_copy(d, p):
        return remote(z_out.at[d, lines(p)], z_in.at[d, lines(p)], z_s.at[d, p], z_r.at[d, p], at(d, False))

    own = pl.ds(pl.multiple_of(core * half, half), half)
    theirs = pl.ds(pl.multiple_of((1 - core) * half, half), half)
    loads = [
        pltpu.make_async_copy(tokens, got.at[0], load.at[0]),
        pltpu.make_async_copy(up.at[0, :, theirs], upv.at[1], load.at[1]),
        pltpu.make_async_copy(up.at[0, :, own], upv.at[0], load.at[2]),
        pltpu.make_async_copy(down.at[0, own, :], downv.at[:half], load.at[3]),
        pltpu.make_async_copy(down.at[0, theirs, :], downv.at[half:], load.at[4]),
    ]
    for copy in loads:
        copy.start()

    barrier = pltpu.get_barrier_semaphore()
    peers = [at(k // 2, k % 2 == 1) for k in range(1, UNITS)] + [core_peer, y_peer]
    for peer in peers:
        pl.semaphore_signal(barrier, inc=1, device_id=peer, device_id_type=MESH)
    pl.semaphore_wait(barrier, len(peers))

    own_x(0).start()
    own_near(0).start()

    @pl.when(is_inner)
    def _():
        own_across(0).start()

    own_x(1).start()
    own_near(1).start()

    @pl.when(is_inner)
    def _():
        own_across(1).start()

    scores = gate[...]
    mix = scores * (ROUTE_SCALE / jnp.sum(scores, axis=0, keepdims=True))
    ids = route[...]
    named = lax.broadcasted_iota(jnp.int32, (UNITS, rows), 0)
    spread = jnp.zeros((UNITS, rows), F32)
    for k in range(UNITS):
        spread = spread + jnp.where(ids[k:k + 1, :] == named, mix[k:k + 1, :], 0.0)
    wt[0] = spread
    for k in range(1, UNITS):
        weight(k).start()
    for copy in loads:
        copy.wait()

    def first_arrivals():
        for p in range(2):
            token_in(1, p).wait_recv()

            @pl.when(is_inner)
            def _():
                near_across(p).start()
                token_in(3, p).wait_recv()
                across_near(p).start()
                second_x(p).start()

            if p == 1:
                near_x(1).start()
            token_in(2, p).wait_recv()

            if p == 0:
                @pl.when(jnp.logical_not(is_inner))
                def _():
                    side_near(0).start()

    def second_arrivals():
        @pl.when(is_inner)
        def _():
            side_near(0).start()

        for p in range(2):
            @pl.when(is_inner)
            def _():
                token_in(6, p).wait_recv()
                far_near(p).start()
                third_x(p).start()

            @pl.when(jnp.logical_not(is_inner))
            def _():
                token_in(3, p).wait_recv()
                second_x(p).start()

    def third_arrivals():
        for p in range(2):
            @pl.when(jnp.logical_not(is_inner))
            def _():
                token_in(6, p).wait_recv()
                third_x(p).start()

    def stage_a(u):
        @pl.when((u == 4) | (u == 5) | (u == 7))
        def _():
            token_in(u, 0).wait_recv()
            token_in(u, 1).wait_recv()

        block = got[u]
        core_out[u] = jnp.dot(block, upv[1], preferred_element_type=F32).astype(BF16)
        core_copy(u).start()
        kept[u] = jnp.dot(block, upv[0], preferred_element_type=F32)

    def stage_b(u):
        core_copy(u).wait_recv()
        total = kept[u] + core_in[u].astype(F32)
        kept[u] = total
        y_out[u] = total.astype(BF16)
        y_copy(u).start()

    def stage_c(u):
        y_copy(u).wait_recv()
        before = kept[u] + y_in[u].astype(F32)
        hid[u, :, :half] = (before / (1.0 + jnp.exp(-before))).astype(BF16)
        hid_copy(u).start()

    def stage_d(u):
        other = (u == 2) | (u == 4) | (u == 5) | (u == 7)
        d = jnp.where((u == 1) | (u == 5), 1, jnp.where((u == 3) | (u == 4), second, third))
        d = jnp.where((u == 0) | (u == 2), 0, d)
        k = 2 * d + other.astype(jnp.int32)

        @pl.when(u >= 1)
        def _():
            weight_in(k).wait_recv()

        scale = jnp.broadcast_to(wt[k, pl.ds(expert, 1), :], (128, rows)).T
        hid_copy(u).wait_recv()
        result = jnp.dot(hid[u], downv[...], preferred_element_type=F32)
        result = result * jnp.concatenate([scale] * (result.shape[1] // 128), axis=1)

        @pl.when((u == 0) | (u == 3) | (u == 6))
        def _():
            acc[d] = result

        @pl.when(u == 1)
        def _():
            z_out[1] = result.astype(BF16)

            @pl.when(jnp.logical_not(is_inner))
            def _():
                z_copy(1, 0).start()
                z_copy(1, 1).start()

        @pl.when(u == 2)
        def _():
            over[0] = result.astype(BF16)

        @pl.when(u == 5)
        def _():
            over[1] = result.astype(BF16)
            over_copy(0).start()
            over_copy(1).start()

        @pl.when((u == 4) | (u == 7))
        def _():
            x_out[d] = result.astype(BF16)
            x_copy(d, 0).start()
            x_copy(d, 1).start()

    def stage_e(d, p):
        x_copy(d, p).wait_recv()
        z_out[d, lines(p)] = (acc[d, lines(p)] + x_in[d, lines(p)].astype(F32)).astype(BF16)
        z_copy(d, p).start()

    def step(t, carry):
        @pl.when(t == 3)
        def _():
            second_arrivals()

        @pl.when(t == 5)
        def _():
            third_arrivals()

        @pl.when(t < UNITS)
        def _():
            stage_a(t)

        @pl.when((t >= 2) & (t < UNITS + 1))
        def _():
            stage_b(t - 1)

        @pl.when((t >= 2) & (t < UNITS + 2))
        def _():
            stage_c(t - 2)

        @pl.when(t == UNITS + 2)
        def _():
            for p in range(2):
                over_copy(p).wait_recv()
                both = over[0, lines(p)].astype(F32) + over[2, lines(p)].astype(F32)
                x_out[0, lines(p)] = both.astype(BF16)
                x_copy(0, p).start()

        @pl.when((t >= 3) & (t < UNITS + 3))
        def _():
            stage_d(t - 3)

        @pl.when((t == 7) & is_inner)
        def _():
            z_copy(1, 0).start()
            z_copy(1, 1).start()

        @pl.when(t == 8)
        def _():
            stage_e(second, 0)
            stage_e(second, 1)

        return carry

    stage_a(0)
    stage_b(0)
    first_arrivals()
    lax.fori_loop(1, UNITS + 3, step, 0)

    for p in range(2):
        for copy in (own_x, own_near, second_x, third_x):
            copy(p).wait_send()
    side_near(0).wait_send()
    near_x(1).wait_send()

    @pl.when(is_inner)
    def _():
        for p in range(2):
            for copy in (own_across, near_across, far_near, across_near):
                copy(p).wait_send()

    for u in range(UNITS):
        if u:
            weight(u).wait_send()
        core_copy(u).wait_send()
        y_copy(u).wait_send()
        hid_copy(u).wait_send()

    for p in range(2):
        stage_e(third, p)

    for p in range(2):
        over_copy(p).wait_send()
        x_copy(2, p).wait_send()
        x_copy(3, p).wait_send()
        for d in range(1, NZ):
            z_copy(d, p).wait_send()

    for p in range(2):
        total = acc[0, lines(p)]
        for d in range(1, NZ):
            z_copy(d, p).wait_recv()
            total = total + z_in[d, lines(p)].astype(F32)
        x_copy(0, p).wait_recv()
        out[lines(p)] = (total + x_in[0, lines(p)].astype(F32)).astype(BF16)
    for p in range(2):
        x_copy(0, p).wait_send()


def dense(tokens, route_ids, gate_scores, up_weight, down_weight):
    rows, features = tokens.shape
    hidden = up_weight.shape[2]
    half = hidden // 2
    vmem = pl.BlockSpec(memory_space=pltpu.VMEM)
    hbm = pl.BlockSpec(memory_space=pltpu.HBM)
    dma = pltpu.SemaphoreType.DMA
    return pl.pallas_call(
        dense_kernel,
        out_shape=jax.ShapeDtypeStruct((rows, features), BF16),
        in_specs=[hbm, vmem, vmem, hbm, hbm],
        out_specs=vmem,
        scratch_shapes=[
            pltpu.VMEM((UNITS, rows, features), BF16),
            pltpu.VMEM((2, features, half), BF16),
            pltpu.VMEM((hidden, features), BF16),
            pltpu.VMEM((UNITS, UNITS, rows), F32),
            pltpu.VMEM((UNITS, rows, half), BF16),
            pltpu.VMEM((UNITS, rows, half), BF16),
            pltpu.VMEM((UNITS, rows, half), F32),
            pltpu.VMEM((UNITS, rows, half), BF16),
            pltpu.VMEM((UNITS, rows, half), BF16),
            pltpu.VMEM((UNITS, rows, hidden), BF16),
            pltpu.VMEM((NZ, rows, features), F32),
            pltpu.VMEM((3, rows, features), BF16),
            pltpu.VMEM((NZ, rows, features), BF16),
            pltpu.VMEM((NZ, rows, features), BF16),
            pltpu.VMEM((NZ, rows, features), BF16),
            pltpu.VMEM((NZ, rows, features), BF16),
        ] + [dma((10, 2)), dma((UNITS, 2))] + [dma((UNITS,))] * 8 + [dma((NZ, 2))] * 4 + [dma((5,))],
        compiler_params=pltpu.CompilerParams(
            collective_id=0, has_side_effects=True, vmem_limit_bytes=63 * 2**20
        ),
        cost_estimate=pl.CostEstimate(
            flops=4 * UNITS * rows * features * hidden,
            bytes_accessed=4 * features * hidden + 4 * rows * features,
            transcendentals=UNITS * rows * half,
        ),
    )(tokens, route_ids.T, gate_scores.T, up_weight, down_weight)


def local(tokens, route_ids, gate_scores, up_weight, down_weight):
    experts = lax.axis_size("expert")
    every = route_ids.shape[1] == experts == UNITS and lax.axis_size("dp") == 4
    body = dense if every and tokens.shape[0] == 128 else routed
    return body(tokens, route_ids, gate_scores, up_weight, down_weight)


def solution(mesh):
    return jax.shard_map(
        local,
        mesh=mesh,
        in_specs=(
            P("expert", "dp"),
            P("expert", None),
            P("expert", None),
            P("expert", "dp", None),
            P("expert", None, "dp"),
        ),
        out_specs=P("expert", "dp"),
        check_vma=False,
    )
```

```python
import functools

import jax
import jax.numpy as jnp
from jax import lax
from jax.experimental import pallas as pl
from jax.experimental.pallas import tpu as pltpu
from jax.sharding import PartitionSpec as P

HOT = 2


ROUTE_SCALE = 2.5


def silu_hidden(before):
    summed = lax.psum(before.astype(jnp.bfloat16), "dp").astype(jnp.float32)
    result = jax.nn.silu(summed).astype(jnp.bfloat16)
    return result


def routed(tokens, route_ids, gate_scores, up_weight, down_weight):
    token_count, chosen_count = route_ids.shape
    features = tokens.shape[1]
    experts = lax.axis_size("expert")
    mean_rows = token_count * chosen_count // experts
    hot_most = min(2 * mean_rows - 1, token_count)
    cold_rows = (experts - HOT) * mean_rows - HOT * (hot_most - mean_rows)
    cold_most = -(-cold_rows // (experts - HOT))
    flat_ids = route_ids.reshape(-1)
    row_total = flat_ids.shape[0]
    expert_range = jnp.arange(experts, dtype=jnp.int32)
    onehot = (flat_ids[:, None] == expert_range[None, :]).astype(jnp.int32)
    running = jnp.cumsum(onehot, axis=0) - 1
    row_ranks = jnp.sum(onehot * running, axis=1)
    padded = jnp.concatenate([tokens, jnp.zeros((1, features), tokens.dtype)], axis=0)
    up_local = up_weight[0]
    down_local = down_weight[0]
    mix_weights = gate_scores * (ROUTE_SCALE / jnp.sum(gate_scores, axis=1, keepdims=True))
    slot_count = max(hot_most, cold_most)
    slot_of_row = flat_ids * slot_count + row_ranks
    slot_table = jnp.full((experts * slot_count,), row_total, jnp.int32)
    slot_table = slot_table.at[slot_of_row].set(jnp.arange(row_total, dtype=jnp.int32), mode="drop")
    sending = padded[slot_table // chosen_count].reshape(experts, slot_count, features)
    arrived = lax.all_to_all(sending, "expert", split_axis=0, concat_axis=0, tiled=True)
    item_count = arrived.shape[1]
    flat_rows = arrived.reshape(-1, features)
    before = jnp.dot(flat_rows, up_local, preferred_element_type=jnp.float32)
    hidden = silu_hidden(before)
    output = jnp.dot(hidden, down_local, preferred_element_type=jnp.float32)
    outcome = output.astype(jnp.bfloat16).reshape(experts, item_count, features)
    returned = lax.all_to_all(outcome, "expert", split_axis=0, concat_axis=0, tiled=True).reshape(
        -1, features
    )
    picked = returned[slot_of_row]
    picked = picked.reshape(token_count, chosen_count, features).astype(jnp.float32)
    mixed = jnp.sum(mix_weights[:, :, None] * picked, axis=1)
    return mixed.astype(jnp.bfloat16)


MESH = pl.DeviceIdType.MESH
F32 = jnp.float32
BF16 = jnp.bfloat16
NZ, NX = 4, 2
UNITS = NZ * NX


def mesh_xor(z, d):
    high = lax.rem(lax.div(z, 2) + lax.div(d, 2), 2)
    low = lax.rem(lax.rem(z, 2) + lax.rem(d, 2), 2)
    return high * 2 + low


def dense_kernel(
    tokens, route, gate, up, down, out,
    got, upv, downv, wt, core_out, core_in, kept, y_out, y_in, hid, acc, over, x_out, x_in, z_out, z_in,
    tok_s, tok_r, w_s, w_r, core_s, core_r, y_s, y_r, hid_s, hid_r, x_s, x_r, z_s, z_r, load,
):
    expert = lax.axis_index("expert")
    part = lax.axis_index("dp")
    z, x = lax.div(expert, NX), lax.rem(expert, NX)
    y, core = lax.div(part, 2), lax.rem(part, 2)
    half = upv.shape[2]
    rows = tokens.shape[0]

    def at(d, other):
        xx = 1 - x if other else x
        return {"expert": mesh_xor(z, d) * NX + xx}

    x_peer = {"expert": z * NX + 1 - x}
    core_peer = {"dp": y * 2 + 1 - core}
    y_peer = {"dp": (1 - y) * 2 + core}

    def remote(src, dst, send, recv, device):
        return pltpu.make_async_remote_copy(
            src_ref=src, dst_ref=dst, send_sem=send, recv_sem=recv,
            device_id=device, device_id_type=MESH,
        )

    inner = lax.rem(mesh_xor(z, lax.div(z, 2)), 2)
    is_inner = inner == 1
    near, across = at(1, False), at(3, False)

    def token(k, src, slot, device):
        def piece(p):
            return remote(
                src.at[lines(p)], got.at[slot, lines(p)], tok_s.at[k, p], tok_r.at[slot, p], device)
        return piece

    def token_in(u, p):
        return remote(tokens.at[lines(p)], got.at[u, lines(p)], tok_s.at[0, p], tok_r.at[u, p], x_peer)

    second, third = 2 + inner, 3 - inner
    own_x = token(0, tokens, 2, x_peer)
    own_near = token(1, tokens, 1, near)
    own_across = token(2, tokens, 3, across)
    near_across = token(3, got.at[1], 5, across)
    side_near = token(4, got.at[2], 6, near)
    across_near = token(5, got.at[3], 3, near)
    far_near = token(6, got.at[5], 5, near)
    second_x = token(7, got.at[3], 4, x_peer)
    third_x = token(8, got.at[5], 7, x_peer)
    near_x = token(9, got.at[1], 6, x_peer)

    def weight(k):
        return remote(wt.at[0], wt.at[k], w_s.at[k], w_r.at[k], at(k // 2, k % 2 == 1))

    def weight_in(u):
        return remote(wt.at[0], wt.at[u], w_s.at[u], w_r.at[u], x_peer)

    def core_copy(u):
        return remote(core_out.at[u], core_in.at[u], core_s.at[u], core_r.at[u], core_peer)

    def y_copy(u, p):
        return remote(y_out.at[u, lines(p)], y_in.at[u, lines(p)], y_s.at[u, p], y_r.at[u, p], y_peer)

    def hid_copy(u):
        return remote(hid.at[u, :, :half], hid.at[u, :, half:], hid_s.at[u], hid_r.at[u], core_peer)

    part_rows = rows // 2

    def lines(p):
        return pl.ds(p * part_rows, part_rows)

    def x_copy(d, p):
        return remote(x_out.at[d, lines(p)], x_in.at[d, lines(p)], x_s.at[d, p], x_r.at[d, p], x_peer)

    def over_copy(p):
        return remote(over.at[1, lines(p)], over.at[2, lines(p)], z_s.at[0, p], z_r.at[0, p], near)

    def z_copy(d, p):
        return remote(z_out.at[d, lines(p)], z_in.at[d, lines(p)], z_s.at[d, p], z_r.at[d, p], at(d, False))

    own = pl.ds(pl.multiple_of(core * half, half), half)
    theirs = pl.ds(pl.multiple_of((1 - core) * half, half), half)
    loads = [
        pltpu.make_async_copy(tokens, got.at[0], load.at[0]),
        pltpu.make_async_copy(up.at[0, :, theirs], upv.at[1], load.at[1]),
        pltpu.make_async_copy(up.at[0, :, own], upv.at[0], load.at[2]),
        pltpu.make_async_copy(down.at[0, own, :], downv.at[:half], load.at[3]),
        pltpu.make_async_copy(down.at[0, theirs, :], downv.at[half:], load.at[4]),
    ]
    for copy in loads:
        copy.start()

    barrier = pltpu.get_barrier_semaphore()
    peers = [at(k // 2, k % 2 == 1) for k in range(1, UNITS)] + [core_peer, y_peer]
    for peer in peers:
        pl.semaphore_signal(barrier, inc=1, device_id=peer, device_id_type=MESH)
    pl.semaphore_wait(barrier, len(peers))

    own_x(0).start()
    own_near(0).start()

    @pl.when(is_inner)
    def _():
        own_across(0).start()

    own_x(1).start()
    own_near(1).start()

    @pl.when(is_inner)
    def _():
        own_across(1).start()

    scores = gate[...]
    mix = scores * (ROUTE_SCALE / jnp.sum(scores, axis=0, keepdims=True))
    ids = route[...]
    named = lax.broadcasted_iota(jnp.int32, (UNITS, rows), 0)
    spread = jnp.zeros((UNITS, rows), F32)
    for k in range(UNITS):
        spread = spread + jnp.where(ids[k:k + 1, :] == named, mix[k:k + 1, :], 0.0)
    wt[0] = spread
    for k in range(1, UNITS):
        weight(k).start()
    for copy in loads:
        copy.wait()

    def first_arrivals():
        for p in range(2):
            token_in(1, p).wait_recv()

            @pl.when(is_inner)
            def _():
                near_across(p).start()
                token_in(3, p).wait_recv()
                across_near(p).start()
                second_x(p).start()

            if p == 1:
                near_x(1).start()
            token_in(2, p).wait_recv()

            if p == 0:
                @pl.when(jnp.logical_not(is_inner))
                def _():
                    side_near(0).start()

    def second_arrivals():
        for p in range(2):
            @pl.when(is_inner)
            def _():
                token_in(5, p).wait_recv()
                far_near(p).start()
                third_x(p).start()

            @pl.when(jnp.logical_not(is_inner))
            def _():
                token_in(3, p).wait_recv()
                second_x(p).start()

        @pl.when(is_inner)
        def _():
            side_near(0).start()

    def third_arrivals():
        for p in range(2):
            @pl.when(jnp.logical_not(is_inner))
            def _():
                token_in(5, p).wait_recv()
                third_x(p).start()

        token_in(4, 0).wait_recv()
        token_in(4, 1).wait_recv()

    def stage_a(u):
        @pl.when(u >= 6)
        def _():
            token_in(u, 0).wait_recv()
            token_in(u, 1).wait_recv()

        block = got[u]
        core_out[u] = jnp.dot(block, upv[1], preferred_element_type=F32).astype(BF16)
        core_copy(u).start()
        kept[u] = jnp.dot(block, upv[0], preferred_element_type=F32)

    def stage_b(u):
        core_copy(u).wait_recv()
        for p in range(2):
            total = kept[u, lines(p)] + core_in[u, lines(p)].astype(F32)
            kept[u, lines(p)] = total
            y_out[u, lines(p)] = total.astype(BF16)
            y_copy(u, p).start()

    def stage_c(u):
        for p in range(2):
            y_copy(u, p).wait_recv()
            before = kept[u, lines(p)] + y_in[u, lines(p)].astype(F32)
            hid[u, lines(p), :half] = (before / (1.0 + jnp.exp(-before))).astype(BF16)
        hid_copy(u).start()

    def stage_d(u):
        other = (u == 2) | (u == 4) | (u >= 6)
        d = jnp.where((u == 1) | (u == 6), 1, jnp.where((u == 3) | (u == 4), second, third))
        d = jnp.where((u == 0) | (u == 2), 0, d)
        k = 2 * d + other.astype(jnp.int32)

        @pl.when(u >= 1)
        def _():
            weight_in(k).wait_recv()

        scale = jnp.broadcast_to(wt[k, pl.ds(expert, 1), :], (128, rows)).T
        hid_copy(u).wait_recv()
        result = jnp.dot(hid[u], downv[...], preferred_element_type=F32)
        result = result * jnp.concatenate([scale] * (result.shape[1] // 128), axis=1)

        @pl.when((u == 0) | (u == 3) | (u == 5))
        def _():
            acc[d] = result

        @pl.when(u == 1)
        def _():
            z_out[1] = result.astype(BF16)

            @pl.when(jnp.logical_not(is_inner))
            def _():
                z_copy(1, 0).start()
                z_copy(1, 1).start()

        @pl.when(u == 2)
        def _():
            over[0] = result.astype(BF16)

        @pl.when(u == 6)
        def _():
            over[1] = result.astype(BF16)
            over_copy(0).start()
            over_copy(1).start()

        @pl.when((u == 4) | (u == 7))
        def _():
            x_out[d] = result.astype(BF16)
            x_copy(d, 0).start()
            x_copy(d, 1).start()

    def stage_e(d, p):
        x_copy(d, p).wait_recv()
        z_out[d, lines(p)] = (acc[d, lines(p)] + x_in[d, lines(p)].astype(F32)).astype(BF16)
        z_copy(d, p).start()

    def step(t, carry):
        @pl.when(t == 3)
        def _():
            second_arrivals()

        @pl.when(t == 4)
        def _():
            third_arrivals()

        @pl.when(t < UNITS)
        def _():
            stage_a(t)

        @pl.when((t >= 2) & (t < UNITS + 1))
        def _():
            stage_b(t - 1)

        @pl.when((t >= 2) & (t < UNITS + 2))
        def _():
            stage_c(t - 2)

        @pl.when((t >= 3) & (t < UNITS + 3))
        def _():
            stage_d(t - 3)

        @pl.when((t == 7) & is_inner)
        def _():
            z_copy(1, 0).start()
            z_copy(1, 1).start()

        @pl.when(t == 8)
        def _():
            stage_e(second, 0)
            stage_e(second, 1)

        return carry

    stage_a(0)
    stage_b(0)
    first_arrivals()
    lax.fori_loop(1, UNITS + 3, step, 0)

    for p in range(2):
        for copy in (own_x, own_near, second_x, third_x):
            copy(p).wait_send()
    side_near(0).wait_send()
    near_x(1).wait_send()

    @pl.when(is_inner)
    def _():
        for p in range(2):
            for copy in (own_across, near_across, far_near, across_near):
                copy(p).wait_send()

    for u in range(UNITS):
        if u:
            weight(u).wait_send()
        core_copy(u).wait_send()
        y_copy(u, 0).wait_send()
        y_copy(u, 1).wait_send()
        hid_copy(u).wait_send()

    for p in range(2):
        stage_e(third, p)
        over_copy(p).wait_recv()
        x_out[0, lines(p)] = (over[0, lines(p)].astype(F32) + over[2, lines(p)].astype(F32)).astype(BF16)
        x_copy(0, p).start()

    for p in range(2):
        over_copy(p).wait_send()
        x_copy(2, p).wait_send()
        x_copy(3, p).wait_send()
        for d in range(1, NZ):
            z_copy(d, p).wait_send()

    for p in range(2):
        total = acc[0, lines(p)]
        for d in range(1, NZ):
            z_copy(d, p).wait_recv()
            total = total + z_in[d, lines(p)].astype(F32)
        x_copy(0, p).wait_recv()
        out[lines(p)] = (total + x_in[0, lines(p)].astype(F32)).astype(BF16)
    for p in range(2):
        x_copy(0, p).wait_send()


def dense(tokens, route_ids, gate_scores, up_weight, down_weight):
    rows, features = tokens.shape
    hidden = up_weight.shape[2]
    half = hidden // 2
    vmem = pl.BlockSpec(memory_space=pltpu.VMEM)
    hbm = pl.BlockSpec(memory_space=pltpu.HBM)
    dma = pltpu.SemaphoreType.DMA
    return pl.pallas_call(
        dense_kernel,
        out_shape=jax.ShapeDtypeStruct((rows, features), BF16),
        in_specs=[hbm, vmem, vmem, hbm, hbm],
        out_specs=vmem,
        scratch_shapes=[
            pltpu.VMEM((UNITS, rows, features), BF16),
            pltpu.VMEM((2, features, half), BF16),
            pltpu.VMEM((hidden, features), BF16),
            pltpu.VMEM((UNITS, UNITS, rows), F32),
            pltpu.VMEM((UNITS, rows, half), BF16),
            pltpu.VMEM((UNITS, rows, half), BF16),
            pltpu.VMEM((UNITS, rows, half), F32),
            pltpu.VMEM((UNITS, rows, half), BF16),
            pltpu.VMEM((UNITS, rows, half), BF16),
            pltpu.VMEM((UNITS, rows, hidden), BF16),
            pltpu.VMEM((NZ, rows, features), F32),
            pltpu.VMEM((3, rows, features), BF16),
            pltpu.VMEM((NZ, rows, features), BF16),
            pltpu.VMEM((NZ, rows, features), BF16),
            pltpu.VMEM((NZ, rows, features), BF16),
            pltpu.VMEM((NZ, rows, features), BF16),
        ] + [dma((10, 2)), dma((UNITS, 2))] + [dma((UNITS,))] * 4 + [dma((UNITS, 2))] * 2 + [dma((UNITS,))] * 2 + [dma((NZ, 2))] * 4 + [dma((5,))],
        compiler_params=pltpu.CompilerParams(
            collective_id=0, has_side_effects=True, vmem_limit_bytes=63 * 2**20
        ),
        cost_estimate=pl.CostEstimate(
            flops=4 * UNITS * rows * features * hidden,
            bytes_accessed=4 * features * hidden + 4 * rows * features,
            transcendentals=UNITS * rows * half,
        ),
    )(tokens, route_ids.T, gate_scores.T, up_weight, down_weight)


def local(tokens, route_ids, gate_scores, up_weight, down_weight):
    experts = lax.axis_size("expert")
    every = route_ids.shape[1] == experts == UNITS and lax.axis_size("dp") == 4
    body = dense if every and tokens.shape[0] == 128 else routed
    return body(tokens, route_ids, gate_scores, up_weight, down_weight)


def solution(mesh):
    return jax.shard_map(
        local,
        mesh=mesh,
        in_specs=(
            P("expert", "dp"),
            P("expert", None),
            P("expert", None),
            P("expert", "dp", None),
            P("expert", None, "dp"),
        ),
        out_specs=P("expert", "dp"),
        check_vma=False,
    )
```
